32 devices in a mesh: stream: 2 (over x), wide: 8 (over z, y), narrow: 2 (over core).
Axes of the slice: x: 2, y: 2, z: 4, core: 2. Of those that a mesh axis runs over, the one named last changes fastest.
Arguments:
- frames: bfloat16 [2, 64, 13, 13, 256], P('stream', ('wide', 'narrow')), may hold values from -6 to 6
- weight3: bfloat16 [2, 2304, 512], P('stream'), may hold values from -0.125 to 0.125
- bias3: bfloat16 [2, 512], P('stream'), may hold values from -3 to 3
- weight4: bfloat16 [2, 4608, 512], P('stream'), may hold values from -0.125 to 0.125
- bias4: bfloat16 [2, 512], P('stream'), may hold values from -3 to 3
- cotangent: bfloat16 [2, 64, 13, 13, 512], P('stream', ('wide', 'narrow')), may hold values from -6 to 6
- clip_counts: int32 [8], replicated, may hold values from 1 to 25, 64 in all
Outputs:
- activations: bfloat16 [2, 64, 13, 13, 512], P('stream', ('wide', 'narrow'))
- frames_grad: bfloat16 [2, 64, 13, 13, 256], P('stream', ('wide', 'narrow'))
- weight3_grad: float32 [2, 2304, 512], P('stream')
- bias3_grad: float32 [2, 512], P('stream')
- weight4_grad: float32 [2, 4608, 512], P('stream')
- bias4_grad: float32 [2, 512], P('stream')
The draws below stay inside these ranges and needn't reach their ends.
Inputs may be any that keep to these rules, and one draw needn't show every extreme that they name: `clip_counts`: the counts sum to 64; the largest is exactly 25.
All inputs are finite; a program needn't handle non-finite values.
Results may differ from the reference program's by a relative error of at most 0.0062.
Values sent between devices are 32-bit elements; how exact they have to be, the bound alone decides.
No kernel may reach another device: no remote copies, remote signals or barrier semaphores. Data moves between devices by JAX's collectives and lax.ppermute only.
A program may use at most 128 MiB of HBM per device.

```python
import math
import jax
import jax.numpy as jnp
import numpy as np
from jax import lax

C_IN = 256
C_MID = 512
C_OUT = 512
SIDE = 13
FRAMES = 64
VIDEOS = 8


def block_scale(stream_key, dims, pieces, least, top_value):
    def one(axis_at, parts):
        steps = jax.random.uniform(jax.random.fold_in(jax.random.fold_in(stream_key, 6), axis_at), (parts,), jnp.float32, least / len(pieces), top_value / len(pieces))
        return jnp.repeat(jnp.exp(steps), dims[axis_at] // parts).reshape((-1,) + (1,) * (len(dims) - axis_at - 1))

    loudness = one(*pieces[0])
    for cut in pieces[1:]:
        loudness = loudness * one(*cut)
    return loudness


def split_up(amount, total, reach, slope):
    portions = [(1 << 20) // math.isqrt(grade ** slope) + 1 for grade in range(2, amount + 1)]
    rest, given = total - reach - (amount - 1), [1] * (amount - 1)
    while rest > 0:
        free = [i for i in range(amount - 1) if given[i] < reach]
        pool, budget = sum([portions[i] for i in free]), rest
        for i in free:
            addition = min(reach - given[i], max(1, budget * portions[i] // pool), rest)
            given[i] = given[i] + addition
            rest = rest - addition
    return np.array([reach] + given)


def uneven_parts(rng, number_of, total, most, lean):
    if number_of == 2:
        one = jax.random.randint(rng, (), max(1, total - most), min(most, total - 1) + 1)
        return jnp.stack([one, total - one])
    sizes = jnp.asarray(split_up(number_of, total, most, lean), jnp.int32)
    twos = (number_of - 1) // 2
    donor, sink = sizes[1:1 + 2 * twos:2], sizes[2:2 + 2 * twos:2]
    margin = jnp.minimum(donor - 1, most - sink)
    shifted = jax.random.randint(jax.random.fold_in(rng, 1), (twos,), 0, 1 << 20) % (margin + 1)
    sizes = sizes.at[1:1 + 2 * twos:2].set(donor - shifted).at[2:2 + 2 * twos:2].set(sink + shifted)
    return sizes[jax.random.permutation(jax.random.fold_in(rng, 2), number_of)]


def centred(own_key, extent, scale, reach, pieces=(), held_as=jnp.bfloat16):
    result = scale * jax.random.normal(own_key, extent, jnp.float32)
    if pieces:
        result = result * block_scale(own_key, extent, pieces, -0.22, 0.18)
    return jnp.clip(result, -reach, reach).astype(held_as)


def setup_inputs(seed: int = 0) -> dict:
    key_of = jax.random.split(jax.random.key(seed), 8)
    return {
        "frames": centred(key_of[0], (2, FRAMES, SIDE, SIDE, C_IN), 1.0, 6.0, ((0, 2), (1, 16))),
        "weight3": centred(key_of[1], (2, 9 * C_IN, C_MID), (9 * C_IN) ** -0.5, 0.125, ((0, 2),)),
        "bias3": centred(key_of[2], (2, C_MID), 0.5, 3.0, ((0, 2),)),
        "weight4": centred(key_of[3], (2, 9 * C_MID, C_OUT), (9 * C_MID // 2) ** -0.5, 0.125, ((0, 2),)),
        "bias4": centred(key_of[4], (2, C_OUT), 0.5, 3.0, ((0, 2),)),
        "cotangent": centred(key_of[5], (2, FRAMES, SIDE, SIDE, C_OUT), 1.0, 6.0, ((0, 2), (1, 16))),
        "clip_counts": uneven_parts(key_of[6], VIDEOS, FRAMES, 25, 2).astype(jnp.int32),
    }


@jax.custom_vjp
def low(v):
    return lax.optimization_barrier(v.astype(jnp.bfloat16)).astype(jnp.float32)

@jax.custom_vjp
def low_back(v):
    return v

def low_keep(v):
    return (low(v), None)

def low_pass(kept, grad):
    return (grad,)

def back_keep(v):
    return (v, None)

def back_low(kept, grad):
    return (low(grad),)
low.defvjp(low_keep, low_pass)
low_back.defvjp(back_keep, back_low)

def convolve(field, weight, c_in, c_out):
    kernel = weight.reshape(3, 3, c_in, c_out)
    return lax.conv_general_dilated(field, kernel, (1, 1), ((1, 1), (1, 1)), dimension_numbers=('NHWC', 'HWIO', 'NHWC'), precision=lax.Precision.HIGHEST)

def forward(field, weight3, bias3, weight4, bias4):
    pre3 = low_back(convolve(field, weight3, C_IN, C_MID) + bias3)
    act3 = low(jax.nn.silu(pre3))
    pre4 = low_back(convolve(act3, weight4, C_MID, C_OUT) + bias4)
    return jax.nn.silu(pre4)

def frame_weights(clip_counts):
    ends = jnp.cumsum(clip_counts)
    starts = ends - clip_counts
    index = jnp.arange(FRAMES, dtype=jnp.int32)
    inside = (index[:, None] >= starts[None, :]) & (index[:, None] < ends[None, :])
    count = lax.optimization_barrier(jnp.sum(jnp.where(inside, clip_counts[None, :], 0), axis=1))
    return FRAMES / (VIDEOS * count.astype(jnp.float32))

def reference(frames, weight3, bias3, weight4, bias4, cotangent, clip_counts):
    scale = frame_weights(clip_counts)
    results = [[], [], [], [], [], []]
    for part in range(2):
        inputs = (frames[part].astype(jnp.float32), weight3[part].astype(jnp.float32), bias3[part].astype(jnp.float32), weight4[part].astype(jnp.float32), bias4[part].astype(jnp.float32))
        output, pullback = jax.vjp(forward, *inputs)
        weighted = cotangent[part].astype(jnp.float32) * scale[:, None, None, None]
        grads = pullback(weighted)
        results[0].append(output.astype(jnp.bfloat16))
        results[1].append(grads[0].astype(jnp.bfloat16))
        results[2].append(grads[1])
        results[3].append(grads[2])
        results[4].append(grads[3])
        results[5].append(grads[4])
    stacked = [jnp.stack(group) for group in results]
    return (stacked[0], stacked[1], stacked[2], stacked[3], stacked[4], stacked[5])
```

```python
import jax
import jax.numpy as jnp
from jax import lax
from jax.sharding import PartitionSpec as P

BF16 = jnp.bfloat16
F32 = jnp.float32


def silu_slope(value):
    sigma = jax.nn.sigmoid(value)
    return sigma * (1.0 + value * (1.0 - sigma))


def convolve(field, weight):
    kernel = weight.reshape(3, 3, field.shape[-1], -1)
    return lax.conv_general_dilated(
        field,
        kernel,
        (1, 1),
        ((1, 1), (1, 1)),
        dimension_numbers=("NHWC", "HWIO", "NHWC"),
        preferred_element_type=F32,
    )


def convolve_back(delta, weight):
    kernel = weight.reshape(3, 3, -1, delta.shape[-1])[::-1, ::-1]
    return lax.conv_general_dilated(
        delta,
        kernel,
        (1, 1),
        ((1, 1), (1, 1)),
        dimension_numbers=("NHWC", "HWOI", "NHWC"),
        preferred_element_type=F32,
    )


def kernel_grad(field, delta, first, count):
    side = field.shape[1]
    low, high = 1 - first, first + count - 2
    grad = lax.conv_general_dilated(
        field,
        delta,
        (1, 1),
        ((low, high), (1, 1)),
        dimension_numbers=("CHWN", "IHWO", "HWNC"),
        preferred_element_type=F32,
    )
    return grad.reshape(-1, delta.shape[-1])


def ring_of(size):
    return list(range(0, size, 2)) + list(range(size - 1, 0, -2))


def ring_pairs(size, way):
    ring = ring_of(size)
    return [(ring[i], ring[(i + way) % size]) for i in range(size)]


def swap_cores(value):
    return lax.ppermute(value, "narrow", [(0, 1), (1, 0)])


def pick(array, index):
    return lax.dynamic_index_in_dim(array, index, 0, keepdims=False)


class Collected:
    def __init__(self, grad, place, size):
        share = lax.psum_scatter(grad, "narrow", scatter_dimension=0, tiled=True)
        share = lax.psum_scatter(share, "wide", scatter_dimension=0, tiled=True)
        share = lax.all_gather(share, "wide", axis=0, tiled=True)
        self.out = lax.all_gather(share, "narrow", axis=0, tiled=True)

    def step(self, number):
        pass

    def result(self):
        return self.out


class Lane:
    def __init__(self, grad, place, size):
        self.size, self.place = size, place
        self.core = lax.axis_index("narrow")
        halves = grad.reshape(2, grad.shape[0] // 2, grad.shape[1])
        mine = pick(halves, self.core) + swap_cores(pick(halves, 1 - self.core))
        self.parts = mine.reshape(size, 2, mine.shape[0] // (2 * size), mine.shape[1])
        self.out = jnp.zeros((2,) + self.parts.shape, F32)
        self.held = [self.chunk(-1, 0), self.chunk(1, 1)]

    def chunk(self, offset, way):
        return pick(self.parts, lax.rem(self.place + offset + self.size, self.size))[way]

    def keep(self, offset, way):
        index = lax.rem(self.place + offset + 2 * self.size, self.size)
        for core, piece in ((self.core, self.held[way]), (1 - self.core, swap_cores(self.held[way]))):
            self.out = lax.dynamic_update_slice(
                self.out, piece[None, None, None], (core, index, way, 0, 0)
            )

    def step(self, number):
        gathering = number >= self.size - 1
        if number == self.size - 1:
            self.keep(0, 0)
            self.keep(0, 1)
        for way in range(2):
            sign = 1 - 2 * way
            got = lax.ppermute(self.held[way], "wide", ring_pairs(self.size, sign))
            if gathering:
                self.held[way] = got
                self.keep(-sign * (number - self.size + 2), way)
            else:
                self.held[way] = got + self.chunk(-sign * (number + 2), way)

    def result(self):
        return self.out.reshape(-1, self.out.shape[-1])


def butterfly(value, size):
    value = value + swap_cores(value)
    reach = 1
    while reach < size:
        value = value + lax.ppermute(value, "wide", [(i, i ^ reach) for i in range(size)])
        reach *= 2
    return value


def body(frames, weight3, bias3, weight4, bias4, cotangent, clip_counts):
    field = frames[0]
    count = field.shape[0]
    w_three, w_four = (weight3[0], weight4[0])
    size = lax.axis_size("wide")
    total_frames = count * size * lax.axis_size("narrow")
    videos = clip_counts.shape[0]
    first = lax.axis_index(("wide", "narrow")) * count
    index = first + jnp.arange(count, dtype=jnp.int32)
    ends = jnp.cumsum(clip_counts)
    starts = ends - clip_counts
    inside = (index[:, None] >= starts[None, :]) & (index[:, None] < ends[None, :])
    owned = jnp.sum(jnp.where(inside, clip_counts[None, :], 0), axis=1)
    scale = total_frames / (videos * owned.astype(F32))
    where = jnp.argsort(jnp.array(ring_of(size), dtype=jnp.int32))
    place = pick(where, lax.axis_index("wide"))

    pre3 = convolve(field, w_three) + bias3[0].astype(F32)
    act3 = jax.nn.silu(pre3).astype(BF16)
    pre4 = convolve(act3, w_four) + bias4[0].astype(F32)
    output = jax.nn.silu(pre4).astype(BF16)
    weighted = cotangent[0].astype(F32) * scale[:, None, None, None]
    delta4 = (weighted * silu_slope(pre4)).astype(BF16)
    reducer = Lane if size <= 8 else Collected
    lanes = [
        reducer(kernel_grad(act3, delta4, 0, 1), place, size),
        reducer(kernel_grad(act3, delta4, 1, 2), place, size),
    ]
    back3 = convolve_back(delta4, w_four)
    delta3 = (back3 * silu_slope(pre3)).astype(BF16)
    lanes.append(reducer(kernel_grad(field, delta3, 0, 3), place, size))
    field_grad = convolve_back(delta3, w_three).astype(BF16)
    biases = jnp.stack(
        [jnp.sum(delta3, axis=(0, 1, 2), dtype=F32), jnp.sum(delta4, axis=(0, 1, 2), dtype=F32)]
    )
    biases = butterfly(biases, size)
    for number in range(2 * (size - 1)):
        for lane in lanes:
            lane.step(number)
    return (
        output[None],
        field_grad[None],
        lanes[2].result()[None],
        biases[0][None],
        jnp.concatenate([lanes[0].result(), lanes[1].result()])[None],
        biases[1][None],
    )


def solution(mesh):
    return jax.shard_map(
        body,
        mesh=mesh,
        in_specs=(
            P("stream", ("wide", "narrow"), None, None, None),
            P("stream", None, None),
            P("stream", None),
            P("stream", None, None),
            P("stream", None),
            P("stream", ("wide", "narrow"), None, None, None),
            P(),
        ),
        out_specs=(
            P("stream", ("wide", "narrow"), None, None, None),
            P("stream", ("wide", "narrow"), None, None, None),
            P("stream", None, None),
            P("stream", None),
            P("stream", None, None),
            P("stream", None),
        ),
        check_vma=False,
    )
```

```python
import jax
import jax.numpy as jnp
from jax import lax
from jax.sharding import PartitionSpec as P

BF16 = jnp.bfloat16
F32 = jnp.float32


def silu_slope(value):
    sigma = jax.nn.sigmoid(value)
    return sigma * (1.0 + value * (1.0 - sigma))


def convolve(field, weight):
    kernel = weight.reshape(3, 3, field.shape[-1], -1)
    return lax.conv_general_dilated(
        field,
        kernel,
        (1, 1),
        ((1, 1), (1, 1)),
        dimension_numbers=("NHWC", "HWIO", "NHWC"),
        preferred_element_type=F32,
    )


def convolve_back(delta, weight):
    kernel = weight.reshape(3, 3, -1, delta.shape[-1])[::-1, ::-1]
    return lax.conv_general_dilated(
        delta,
        kernel,
        (1, 1),
        ((1, 1), (1, 1)),
        dimension_numbers=("NHWC", "HWOI", "NHWC"),
        preferred_element_type=F32,
    )


def kernel_grad(field, delta):
    grad = lax.conv_general_dilated(
        field,
        delta,
        (1, 1),
        ((1, 1), (1, 1)),
        dimension_numbers=("CHWN", "IHWO", "HWNC"),
        preferred_element_type=F32,
    )
    return grad.reshape(9, field.shape[-1], delta.shape[-1])


def swap_cores(value):
    return lax.ppermute(value, "narrow", [(0, 1), (1, 0)])


def pick(array, index, axis=0):
    return lax.dynamic_index_in_dim(array, index, axis, keepdims=False)


class Ring:
    def __init__(self, size):
        self.size = size
        order = list(range(0, size, 2)) + list(range(size - 1, 0, -2))
        self.pairs = []
        for core, way in ((0, 1), (1, -1)):
            for i in range(size):
                self.pairs.append((2 * order[i] + core, 2 * order[(i + way) % size] + core))
        wide = lax.axis_index("wide")
        self.core = lax.axis_index("narrow")
        half = wide // 2
        self.place = jnp.where(wide % 2 == 0, half, size - 1 - half)
        self.way = 1 - 2 * self.core

    def send(self, value):
        return lax.ppermute(value, ("wide", "narrow"), self.pairs)

    def chunk(self, back):
        return lax.rem(self.place - self.way * back + 2 * self.size, self.size)


class Collected:
    def __init__(self, grad, ring):
        flat = grad.reshape(-1, grad.shape[-1])
        share = lax.psum_scatter(flat, "narrow", scatter_dimension=0, tiled=True)
        share = lax.psum_scatter(share, "wide", scatter_dimension=0, tiled=True)
        share = lax.all_gather(share, "wide", axis=0, tiled=True)
        self.out = lax.all_gather(share, "narrow", axis=0, tiled=True).reshape(grad.shape)

    def step(self, number):
        pass

    def result(self):
        return self.out


class Lane:
    def __init__(self, grad, ring):
        self.ring = ring
        taps, rows, width = grad.shape
        halves = grad.reshape(taps, 2, rows // 2, width)
        self.piece = rows // (2 * ring.size)
        self.parts = pick(halves, ring.core, 1) + swap_cores(pick(halves, 1 - ring.core, 1))
        self.out = jnp.zeros(grad.shape, F32)
        self.held = self.own(1)

    def own(self, back):
        start = self.ring.chunk(back) * self.piece
        return lax.dynamic_slice_in_dim(self.parts, start, self.piece, 1)

    def keep(self, back):
        half = self.parts.shape[1]
        mine, theirs = self.ring.core * half, (1 - self.ring.core) * half
        other = lax.rem(self.ring.place + self.ring.way * back + 2 * self.ring.size, self.ring.size)
        for piece, start in (
            (self.held, mine + self.ring.chunk(back) * self.piece),
            (swap_cores(self.held), theirs + other * self.piece),
        ):
            self.out = lax.dynamic_update_slice(self.out, piece, (0, start, 0))

    def step(self, number):
        last = self.ring.size - 1
        if number == last:
            self.keep(0)
        got = self.ring.send(self.held)
        if number < last:
            self.held = got + self.own(number + 2)
        else:
            self.held = got
            self.keep(number - last + 1)

    def result(self):
        return self.out


def butterfly(value, size):
    value = value + swap_cores(value)
    reach = 1
    while reach < size:
        value = value + lax.ppermute(value, "wide", [(i, i ^ reach) for i in range(size)])
        reach *= 2
    return value


def body(frames, weight3, bias3, weight4, bias4, cotangent, clip_counts):
    field = frames[0]
    count = field.shape[0]
    w_three, w_four = (weight3[0], weight4[0])
    size = lax.axis_size("wide")
    total_frames = count * size * lax.axis_size("narrow")
    videos = clip_counts.shape[0]
    first = lax.axis_index(("wide", "narrow")) * count
    index = first + jnp.arange(count, dtype=jnp.int32)
    video = jnp.arange(videos, dtype=jnp.int32)
    before = video[:, None] < video[None, :]
    starts = jnp.sum(jnp.where(before, clip_counts[:, None], 0), axis=0)
    ends = starts + clip_counts
    inside = (index[:, None] >= starts[None, :]) & (index[:, None] < ends[None, :])
    owned = jnp.sum(jnp.where(inside, clip_counts[None, :], 0), axis=1)
    scale = total_frames / (videos * owned.astype(F32))
    ring = Ring(size)

    pre3 = convolve(field, w_three) + bias3[0].astype(F32)
    act3 = jax.nn.silu(pre3).astype(BF16)
    pre4 = convolve(act3, w_four) + bias4[0].astype(F32)
    output = jax.nn.silu(pre4).astype(BF16)
    weighted = cotangent[0].astype(F32) * scale[:, None, None, None]
    delta4 = (weighted * silu_slope(pre4)).astype(BF16)
    reducer = Lane if size <= 8 else Collected
    half = act3.shape[-1] // 2
    lanes = [
        reducer(kernel_grad(act3[..., :half], delta4), ring),
        reducer(kernel_grad(act3[..., half:], delta4), ring),
    ]
    back3 = convolve_back(delta4, w_four)
    delta3 = (back3 * silu_slope(pre3)).astype(BF16)
    lanes.append(reducer(kernel_grad(field, delta3), ring))
    field_grad = convolve_back(delta3, w_three).astype(BF16)
    biases = jnp.stack(
        [jnp.sum(delta3, axis=(0, 1, 2), dtype=F32), jnp.sum(delta4, axis=(0, 1, 2), dtype=F32)]
    )
    biases = butterfly(biases, size)
    for number in range(2 * (size - 1)):
        for lane in lanes:
            lane.step(number)
    return (
        output[None],
        field_grad[None],
        lanes[2].result().reshape(w_three.shape)[None],
        biases[0][None],
        jnp.concatenate([lanes[0].result(), lanes[1].result()], 1).reshape(w_four.shape)[None],
        biases[1][None],
    )


def solution(mesh):
    return jax.shard_map(
        body,
        mesh=mesh,
        in_specs=(
            P("stream", ("wide", "narrow"), None, None, None),
            P("stream", None, None),
            P("stream", None),
            P("stream", None, None),
            P("stream", None),
            P("stream", ("wide", "narrow"), None, None, None),
            P(),
        ),
        out_specs=(
            P("stream", ("wide", "narrow"), None, None, None),
            P("stream", ("wide", "narrow"), None, None, None),
            P("stream", None, None),
            P("stream", None),
            P("stream", None, None),
            P("stream", None),
        ),
        check_vma=False,
    )
```

```python
import functools

import jax
import jax.numpy as jnp
from jax import lax
from jax.experimental import pallas as pl
from jax.experimental.pallas import tpu as pltpu
from jax.sharding import PartitionSpec as P

BF16 = jnp.bfloat16
F32 = jnp.float32
STEP = 16
MIB = 1024 * 1024
HEAD_MIB, BACK4_MIB, BACK3_MIB = 60, 62, 16
HBM = pl.BlockSpec(memory_space=pltpu.HBM)


def own_place(size):
    core, wide = lax.axis_index("narrow"), lax.axis_index("wide")
    half = lax.div(wide, 2)
    return core, jnp.where(lax.rem(wide, 2) == 0, half, size - 1 - half), 1 - 2 * core


def kernel_call(kernel, outs, scratch, mib, flops, *args, aliases={}):
    return pl.pallas_call(
        kernel,
        out_shape=outs,
        in_specs=[HBM] * len(args),
        out_specs=jax.tree.map(lambda _: HBM, outs),
        scratch_shapes=scratch,
        input_output_aliases=aliases,
        compiler_params=pltpu.CompilerParams(vmem_limit_bytes=mib * MIB),
        cost_estimate=pl.CostEstimate(flops=flops, bytes_accessed=8 * MIB, transcendentals=0),
    )(*args)


def spread(value, cat_ref, count):
    rows, width = value.shape
    edge = count * STEP
    for at, shift in enumerate((count, 0, rows - count)):
        moved = value if shift == 0 else pltpu.roll(value, shift, 0)
        cat_ref[edge : edge + rows, at * width : (at + 1) * width] = moved.astype(BF16)


def clear_edges(cat_ref, count):
    edge = count * STEP
    zeros = jnp.zeros((edge, cat_ref.shape[1]), cat_ref.dtype)
    cat_ref[0:edge, :] = zeros
    cat_ref[cat_ref.shape[0] - edge :, :] = zeros


def convolve_into(acc_ref, cat_ref, w_ref, edge):
    rows, width = acc_ref.shape[0], cat_ref.shape[1]
    for r in range(3):
        part = jnp.dot(
            cat_ref[r * edge : r * edge + rows, :],
            w_ref[r * width : (r + 1) * width, :],
            preferred_element_type=F32,
        )
        if r == 0:
            acc_ref[...] = part
        else:
            acc_ref[...] += part


def back_into(acc_ref, cat_ref, w_ref, edge):
    rows, width = acc_ref.shape[0], w_ref.shape[2]
    for r in range(3):
        for c in range(3):
            part = lax.dot_general(
                cat_ref[(2 - r) * edge : (2 - r) * edge + rows, (2 - c) * width : (3 - c) * width],
                w_ref[3 * r + c],
                (((1,), (1,)), ((), ())),
                preferred_element_type=F32,
            )
            if r + c == 0:
                acc_ref[...] = part
            else:
                acc_ref[...] += part


def silu_slope(value, sigma):
    return sigma * (1.0 + value * (1.0 - sigma))


def head_kernel(
    total, counts_hbm, frames_hbm, w3_hbm, b3_hbm, w4_hbm, b4_hbm, cot_hbm,
    out_hbm, mine_hbm, slope_hbm, field_mine_hbm, send_hbm,
    counts_ref, frames_ref, w3_ref, b3_ref, w4_ref, b4_ref, cot_ref,
    field_ref, act_ref, acc_ref, slope_ref, delta_ref, out_ref, block3_ref, block_ref, cat3_ref, cat4_ref,
    in_sems, out_sems,
):
    sources = (frames_hbm, counts_hbm, w3_hbm, b3_hbm, b4_hbm, w4_hbm, cot_hbm)
    targets = (frames_ref, counts_ref, w3_ref, b3_ref, b4_ref, w4_ref, cot_ref)
    loads = [
        pltpu.make_async_copy(source, target, in_sems.at[at])
        for at, (source, target) in enumerate(zip(sources, targets))
    ]
    for load in loads:
        load.start()
    side, count = frames_ref.shape[0], frames_ref.shape[2]
    edge = count * STEP
    valid = side * count
    videos = counts_ref.shape[0]
    half3, half4 = field_mine_hbm.shape[1], mine_hbm.shape[1]
    c_out = delta_ref.shape[1]
    delta_hbm = send_hbm.at[:, 0:c_out]

    block3_ref[...] = jnp.zeros_like(block3_ref)
    block_ref[...] = jnp.zeros_like(block_ref)
    clear_edges(cat3_ref, count)
    clear_edges(cat4_ref, count)
    for load in loads[:2]:
        load.wait()

    def gather(i, _):
        for j in range(side):
            block3_ref[j * count : (j + 1) * count, :] = frames_ref[i, j].astype(F32)
        field_ref[pl.ds(pl.multiple_of(i * edge, edge), edge), :] = block3_ref[...]
        return 0

    lax.fori_loop(0, side, gather, 0)
    spread(field_ref[...], cat3_ref, count)
    core = lax.axis_index("narrow")
    first = (lax.axis_index("wide") * lax.axis_size("narrow") + core) * count

    def part(at, half):
        return pl.ds(pl.multiple_of(at * half, half), half)

    stores = [
        pltpu.make_async_copy(field_ref.at[:, part(core, half3)], field_mine_hbm, out_sems.at[0]),
        pltpu.make_async_copy(field_ref.at[:, part(1 - core, half3)], send_hbm.at[:, c_out + half4 :], out_sems.at[1]),
    ]

    def owned(f):
        index = first + f

        def look(v, carry):
            start, found = carry
            end = start + counts_ref[v]
            inside = jnp.logical_and(index >= start, index < end)
            return end, jnp.where(inside, counts_ref[v], found)

        return lax.fori_loop(0, videos, look, (jnp.int32(0), jnp.int32(1)))[1]

    row = lax.broadcasted_iota(jnp.int32, (edge, 1), 0)
    held = jnp.zeros((edge, 1), jnp.int32)
    for f in range(count):
        held = jnp.where(lax.rem(row, count) == f, owned(f), held)
    scale = total / (videos * held.astype(F32))
    for load in loads[2:5]:
        load.wait()
    convolve_into(acc_ref, cat3_ref, w3_ref, edge)
    bias3 = b3_ref[...].astype(F32)

    def silu_rows(i, _):
        here = pl.ds(pl.multiple_of(i * edge, edge), edge)
        pre = acc_ref[here, :] + bias3
        sigma = jax.nn.sigmoid(pre)
        slope_ref[here, :] = silu_slope(pre, sigma)
        act = jnp.where(row < valid, pre * sigma, 0.0)
        act_ref[here, :] = act.astype(BF16).astype(F32)
        return 0

    lax.fori_loop(0, side, silu_rows, 0)
    stores += [
        pltpu.make_async_copy(act_ref.at[:, part(1 - core, half4)], send_hbm.at[:, c_out : c_out + half4], out_sems.at[2]),
        pltpu.make_async_copy(act_ref.at[:, part(core, half4)], mine_hbm, out_sems.at[3]),
        pltpu.make_async_copy(slope_ref, slope_hbm, out_sems.at[4]),
    ]
    for store in stores:
        store.start()
    spread(act_ref[...], cat4_ref, count)
    for load in loads[5:]:
        load.wait()
    convolve_into(acc_ref, cat4_ref, w4_ref, edge)
    bias4 = b4_ref[...].astype(F32)

    def last_rows(i, _):
        here = pl.ds(pl.multiple_of(i * edge, edge), edge)
        for j in range(side):
            block_ref[j * count : (j + 1) * count, :] = cot_ref[i, j].astype(F32)
        pre = acc_ref[here, :] + bias4
        sigma = jax.nn.sigmoid(pre)
        delta = block_ref[...] * scale * silu_slope(pre, sigma)
        delta_ref[here, :] = delta.astype(BF16).astype(F32)
        pltpu.make_async_copy(delta_ref.at[here], send_hbm.at[here, 0:c_out], out_sems.at[5]).start()
        out = pre * sigma
        for j in range(side):
            out_ref[i, j] = out[j * count : (j + 1) * count, :].astype(BF16)
        return 0

    lax.fori_loop(0, side, last_rows, 0)
    stores.append(pltpu.make_async_copy(out_ref, out_hbm, out_sems.at[6]))
    stores[-1].start()
    stores.append(pltpu.make_async_copy(delta_ref, delta_hbm, out_sems.at[5]))
    for store in stores:
        store.wait()


def head(total, clip_counts, frames, w3, b3, w4, b4, cot):
    side, count, c_in = frames.shape[1:]
    c_mid, c_out = w3.shape[1], w4.shape[1]
    rows = side * count * STEP
    edges = rows + 2 * count * STEP

    def field(width):
        return jax.ShapeDtypeStruct((rows, width), F32)

    return kernel_call(
        functools.partial(head_kernel, float(total)),
        (
            jax.ShapeDtypeStruct(cot.shape, BF16),
            field(c_mid // 2),
            field(c_mid),
            field(c_in // 2),
            field(c_out + c_mid // 2 + c_in // 2),
        ),
        [
            pltpu.SMEM(clip_counts.shape, jnp.int32),
            pltpu.VMEM(frames.shape, BF16),
            pltpu.VMEM(w3.shape, BF16),
            pltpu.VMEM(b3.shape, BF16),
            pltpu.VMEM(w4.shape, BF16),
            pltpu.VMEM(b4.shape, BF16),
            pltpu.VMEM(cot.shape, BF16),
            pltpu.VMEM((rows, c_in), F32),
            pltpu.VMEM((rows, c_mid), F32),
            pltpu.VMEM((rows, c_mid), F32),
            pltpu.VMEM((rows, c_mid), F32),
            pltpu.VMEM((rows, c_out), F32),
            pltpu.VMEM(cot.shape, BF16),
            pltpu.VMEM((count * STEP, c_in), F32),
            pltpu.VMEM((count * STEP, c_out), F32),
            pltpu.VMEM((edges, 3 * c_in), BF16),
            pltpu.VMEM((edges, 3 * c_mid), BF16),
            pltpu.SemaphoreType.DMA((7,)),
            pltpu.SemaphoreType.DMA((7,)),
        ],
        HEAD_MIB,
        2 * rows * 9 * c_mid * (c_in + c_out),
        clip_counts, frames, w3, b3, w4, b4, cot,
    )


def load_columns(pieces, target, sem):
    copies, at = [], 0
    for piece in pieces:
        width = piece.shape[1]
        copies.append(pltpu.make_async_copy(piece, target.at[:, at : at + width], sem.at[len(copies)]))
        at += width
    for copy in copies:
        copy.start()
    return copies


def back4_kernel(
    count, delta_hbm, slope_hbm, w_hbm, out_hbm, sums_hbm,
    delta_ref, slope_ref, w_ref, cat_ref, acc_ref, out_ref, sums_ref, sems,
):
    edge = count * STEP
    rows = out_ref.shape[0]
    loads = [
        pltpu.make_async_copy(delta_hbm.at[:, 0 : delta_ref.shape[1]], delta_ref, sems.at[0]),
        pltpu.make_async_copy(w_hbm, w_ref, sems.at[1]),
        pltpu.make_async_copy(slope_hbm, slope_ref, sems.at[2]),
    ]
    for load in loads:
        load.start()
    clear_edges(cat_ref, count)
    loads[0].wait()
    spread(delta_ref[...], cat_ref, count)
    loads[1].wait()
    back_into(acc_ref, cat_ref, w_ref, edge)
    loads[2].wait()
    side = rows // edge
    valid = lax.broadcasted_iota(jnp.int32, (edge, 1), 0) < side * count

    def rows_of(i, carry):
        here = pl.ds(pl.multiple_of(i * edge, edge), edge)
        delta = jnp.where(valid, acc_ref[here, :] * slope_ref[here, :], 0.0)
        delta = delta.astype(BF16).astype(F32)
        out_ref[here, :] = delta
        pltpu.make_async_copy(out_ref.at[here], out_hbm.at[here], sems.at[3]).start()
        sum3, sum4 = carry
        return (
            sum3 + jnp.sum(delta, 0, keepdims=True),
            sum4 + jnp.sum(delta_ref[here, :], 0, keepdims=True),
        )

    nothing = (jnp.zeros((1, out_ref.shape[1]), F32), jnp.zeros((1, delta_ref.shape[1]), F32))
    sums_ref[0:1, :], sums_ref[1:2, :] = lax.fori_loop(0, side, rows_of, nothing)
    stores = [
        pltpu.make_async_copy(out_ref, out_hbm, sems.at[3]),
        pltpu.make_async_copy(sums_ref, sums_hbm, sems.at[4]),
    ]
    stores[1].start()
    for store in stores:
        store.wait()


def back4(count, delta, slope, w):
    rows = delta.shape[0]
    taps, c_mid, width = w.shape
    return kernel_call(
        functools.partial(back4_kernel, count),
        (jax.ShapeDtypeStruct((rows, c_mid), F32), jax.ShapeDtypeStruct((2, width), F32)),
        [
            pltpu.VMEM((rows, width), F32),
            pltpu.VMEM((rows, c_mid), F32),
            pltpu.VMEM((taps, c_mid, width), BF16),
            pltpu.VMEM((rows + 2 * count * STEP, 3 * width), BF16),
            pltpu.VMEM((rows, c_mid), F32),
            pltpu.VMEM((rows, c_mid), F32),
            pltpu.VMEM((2, width), F32),
            pltpu.SemaphoreType.DMA((5,)),
        ],
        BACK4_MIB,
        2 * rows * c_mid * width * taps,
        delta, slope, w,
    )


def back3_kernel(count, pieces, *refs):
    deltas, (w_hbm, out_hbm, delta_ref, w_ref, cat_ref, acc_ref, out_ref, sems) = refs[:pieces], refs[pieces:]
    edge = count * STEP
    loads = load_columns(deltas, delta_ref, sems)
    load = pltpu.make_async_copy(w_hbm, w_ref, sems.at[pieces])
    load.start()
    clear_edges(cat_ref, count)
    for copy in loads:
        copy.wait()
    spread(delta_ref[...], cat_ref, count)
    load.wait()
    back_into(acc_ref, cat_ref, w_ref, edge)
    side = out_ref.shape[0]

    def rows_of(i, _):
        block = acc_ref[pl.ds(pl.multiple_of(i * edge, edge), edge), :]
        for j in range(side):
            out_ref[i, j] = block[j * count : (j + 1) * count, :].astype(BF16)
        return 0

    lax.fori_loop(0, side, rows_of, 0)
    store = pltpu.make_async_copy(out_ref, out_hbm, sems.at[pieces + 1])
    store.start()
    store.wait()


def back3(side, count, deltas, w):
    rows = deltas[0].shape[0]
    taps, c_in, width = w.shape
    return kernel_call(
        functools.partial(back3_kernel, count, len(deltas)),
        jax.ShapeDtypeStruct((side, side, count, c_in), BF16),
        [
            pltpu.VMEM((rows, width), F32),
            pltpu.VMEM(w.shape, BF16),
            pltpu.VMEM((rows + 2 * count * STEP, 3 * width), BF16),
            pltpu.VMEM((rows, c_in), F32),
            pltpu.VMEM((side, side, count, c_in), BF16),
            pltpu.SemaphoreType.DMA((len(deltas) + 2,)),
        ],
        BACK3_MIB,
        2 * rows * c_in * width * taps,
        *deltas, w,
    )


def grad_kernel(count, side, lanes, chunks, size, places, tail, *refs):
    sums_hbm, refs = refs[4 : 4 + 2 * tail], refs[:4] + refs[4 + 2 * tail :]
    outs, (*targets, turned_ref, both_ref, acc_ref, sums_ref, in_sems, out_sems) = (
        refs[4 : 4 + 2 * lanes], refs[4 + 2 * lanes :],
    )
    mine_ref, theirs_ref, delta_ref, other_ref = targets
    _, spot, way = own_place(size)
    edge = count * STEP
    wide = 2 * edge
    k = mine_ref.shape[1]
    groups = (0, side // 3, 2 * side // 3, side)
    loads = []
    for group in range(3):
        rows = slice(groups[group] * edge, groups[group + 1] * edge)
        loads.append([])
        for at in range(4):
            columns = slice(places[at], places[at] + targets[at].shape[1])
            copy = pltpu.make_async_copy(
                refs[at].at[rows, columns], targets[at].at[rows], in_sems.at[at, group]
            )
            copy.start()
            loads[-1].append(copy)
    extra = [
        pltpu.make_async_copy(source, sums_ref.at[at], in_sems.at[4, at]) for at, source in enumerate(sums_hbm)
    ]
    for load in extra:
        load.start()
    turned_ref[:, 0:wide] = jnp.zeros((3 * k, wide), BF16)
    turned_ref[:, (side + 1) * wide :] = jnp.zeros((3 * k, wide), BF16)

    def turn(i, carry):
        here = pl.ds(pl.multiple_of(i * edge, edge), edge)
        there = pl.ds(pl.multiple_of((i + 1) * wide, wide), wide)
        turned = jnp.concatenate([mine_ref[here, :], theirs_ref[here, :]], 0).T
        for c, shift in enumerate((count, 0, wide - count)):
            moved = turned if shift == 0 else pltpu.roll(turned, shift, 1)
            turned_ref[c * k : (c + 1) * k, there] = moved.astype(BF16)
        to = pl.multiple_of(i * wide, wide)
        both_ref[pl.ds(to, edge), :] = delta_ref[here, :].astype(BF16)
        both_ref[pl.ds(to + edge, edge), :] = other_ref[here, :].astype(BF16)
        return carry

    for group in range(3):
        for load in loads[group]:
            load.wait()
        lax.fori_loop(groups[group], groups[group + 1], turn, 0)
    blocks = 3 * k // (8 * lanes * chunks)
    if tail:
        for load in extra:
            load.wait()
        acc_ref[0, :, 3 * blocks] = jnp.zeros((chunks,) + acc_ref.shape[3:], F32)
        acc_ref[0, 0, 3 * blocks, 0:2, :] = sums_ref[0] + sums_ref[1]
    stores = []
    for r in range(3):
        part = jnp.dot(
            turned_ref[:, r * wide : (r + side) * wide], both_ref[...], preferred_element_type=F32
        )
        part = part.reshape((3, lanes, chunks, blocks // 3, 8, part.shape[1]))
        for chunk in range(chunks):
            at = lax.rem(way * (spot - chunk) + 2 * size - 1, size) if chunks > 1 else 0
            for lane in range(lanes):
                piece = part[:, lane, chunk].reshape((blocks,) + acc_ref.shape[3:])
                acc_ref[lane, at, r * blocks : (r + 1) * blocks] = piece
        here = slice(r * blocks, (r + 1) * blocks if r < 2 else acc_ref.shape[2])
        for lane in range(lanes):
            first, others = outs[2 * lane : 2 * lane + 2]
            pairs = [(acc_ref.at[lane, 0, here], first.at[here])]
            if chunks > 1:
                pairs.append((acc_ref.at[lane, 1:, here], others.at[:, here]))
            for source, target in pairs:
                copy = pltpu.make_async_copy(source, target, out_sems.at[len(stores)])
                copy.start()
                stores.append(copy)
    for store in stores:
        store.wait()


def grad(mib, side, count, lanes, chunks, size, o, mine, theirs, delta, other, sums=()):
    arrays, places = zip(mine, theirs, delta, other)
    rows, k = arrays[0].shape
    blocks = 9 * k // (8 * lanes * chunks) + (1 if sums else 0)
    first = jax.ShapeDtypeStruct((blocks, 8, o), F32)
    others = jax.ShapeDtypeStruct((max(chunks - 1, 1), blocks, 8, o), F32)
    results = kernel_call(
        functools.partial(grad_kernel, count, side, lanes, chunks, size, places, bool(sums)),
        (first, others) * lanes,
        [
            pltpu.VMEM((rows, k), F32),
            pltpu.VMEM((rows, k), F32),
            pltpu.VMEM((rows, o), F32),
            pltpu.VMEM((rows, o), F32),
            pltpu.VMEM((3 * k, 2 * count * STEP * (side + 2)), BF16),
            pltpu.VMEM((2 * rows, o), BF16),
            pltpu.VMEM((lanes, chunks, blocks, 8, o), F32),
            pltpu.VMEM((2, 2, o), F32),
            pltpu.SemaphoreType.DMA((5, 3)),
            pltpu.SemaphoreType.DMA((6 * lanes,)),
        ],
        mib,
        2 * 2 * rows * 9 * k * o,
        *arrays, *sums,
    )
    return [(results[2 * lane], results[2 * lane + 1]) for lane in range(lanes)]


def lay_kernel(layout, size, inputs, *refs):
    outs, sems = refs[inputs:-1], refs[-1]
    core, spot, way = own_place(size)
    copies = []
    for at, (out, low, stride, back, own) in enumerate(layout):
        rows = refs[at].shape[1]
        chunk = lax.rem(spot - way * (back if own else -back) + 2 * size, size)
        start = low + (core if own else 1 - core) * stride + chunk * rows
        there = outs[out].at[:, pl.ds(pl.multiple_of(start, rows), rows), :]
        copies.append(pltpu.make_async_copy(refs[at], there, sems.at[at]))
    for copy in copies:
        copy.start()
    for copy in copies:
        copy.wait()


def lay(size, pieces, layout, results, shapes):
    kept = [at for at, result in enumerate(results) if result is not None]
    inputs = len(pieces) + len(kept)
    return kernel_call(
        functools.partial(lay_kernel, tuple(layout), size, inputs),
        tuple(jax.ShapeDtypeStruct(shape, F32) for shape in shapes),
        [pltpu.SemaphoreType.DMA((len(pieces),))],
        1,
        0,
        *pieces, *[results[at] for at in kept],
        aliases={len(pieces) + at: out for at, out in enumerate(kept)},
    )


def tally_kernel(size, *refs):
    pieces, (first_hbm, second_hbm, all_ref, total_ref, in_sems, out_sems) = refs[:size], refs[size:]
    _, spot, way = own_place(size)
    loads = []
    for back, piece in enumerate(pieces):
        chunk = lax.rem(spot - way * back + 2 * size, size)
        loads.append(pltpu.make_async_copy(piece.at[piece.shape[0] - 1], all_ref.at[chunk], in_sems.at[back]))
        loads[-1].start()
    for load in loads:
        load.wait()
    total = all_ref[0]
    for chip in range(1, size):
        total = total + all_ref[chip]
    total_ref[0] = total[0:1]
    total_ref[1] = total[1:2]
    stores = [
        pltpu.make_async_copy(total_ref.at[at], out, out_sems.at[at])
        for at, out in enumerate((first_hbm, second_hbm))
    ]
    for store in stores:
        store.start()
    for store in stores:
        store.wait()


def tally(pieces):
    size, width = len(pieces), pieces[0].shape[2]
    out = jax.ShapeDtypeStruct((1, width), F32)
    return kernel_call(
        functools.partial(tally_kernel, size),
        (out, out),
        [
            pltpu.VMEM((size, 8, width), F32),
            pltpu.VMEM((2, 1, width), F32),
            pltpu.SemaphoreType.DMA((size,)),
            pltpu.SemaphoreType.DMA((2,)),
        ],
        2,
        0,
        *pieces,
    )


def swap_cores(value):
    return lax.ppermute(value, "narrow", [(0, 1), (1, 0)])


def pick(array, index, axis=0):
    return lax.dynamic_index_in_dim(array, index, axis, keepdims=False)


class Ring:
    def __init__(self, size):
        self.size = size
        order = list(range(0, size, 2)) + list(range(size - 1, 0, -2))
        self.pairs = []
        for core, way in ((0, 1), (1, -1)):
            for i in range(size):
                self.pairs.append((2 * order[i] + core, 2 * order[(i + way) % size] + core))
        wide = lax.axis_index("wide")
        self.core = lax.axis_index("narrow")
        half = wide // 2
        self.place = jnp.where(wide % 2 == 0, half, size - 1 - half)
        self.way = 1 - 2 * self.core

    def send(self, value):
        return lax.ppermute(value, ("wide", "narrow"), self.pairs)

    def chunk(self, back):
        return lax.rem(self.place - self.way * back + 2 * self.size, self.size)


def collected(grad, core):
    taps, rows, width = grad.shape
    share = lax.psum_scatter(grad.reshape(-1, width), "wide", scatter_dimension=0, tiled=True)
    mine = lax.all_gather(share, "wide", axis=0, tiled=True).reshape(grad.shape)
    theirs = swap_cores(mine)
    lower, upper = jnp.where(core == 0, mine, theirs), jnp.where(core == 0, theirs, mine)
    return jnp.concatenate([lower, upper], 1)


class Lane:
    def __init__(self, parts, ring, low, stride, blocks):
        self.ring, self.low, self.stride, self.blocks = ring, low, stride, blocks
        self.held, self.parts = parts
        self.passed = [self.held]
        self.pieces, self.lows = [], []

    def keep(self, back):
        for piece, own in ((self.held, True), (swap_cores(self.held), False)):
            self.pieces.append(piece.reshape(9, -1, piece.shape[-1]))
            self.lows.append((self.low, self.stride, back, own))

    def step(self, number):
        last = self.ring.size - 1
        if number == last:
            self.keep(0)
        got = self.ring.send(self.held)
        if number < last:
            self.passed.append(got)
            self.held = got + self.parts[number]
            if number == last - 1:
                self.held = self.held[: self.blocks]
        else:
            self.held = got
            self.keep(number - last + 1)


def lay_lanes(lanes, results, shapes):
    pieces, layout = [], []
    for lane, at in lanes:
        pieces += lane.pieces
        layout += [(at,) + low for low in lane.lows]
        size, lane.pieces, lane.lows = lane.ring.size, [], []
    return lay(size, pieces, layout, results, shapes)


def after(value, *others):
    return lax.optimization_barrier((value,) + others)[0]


def body(frames, weight3, bias3, weight4, bias4, cotangent, clip_counts):
    count, side, c_in = frames.shape[1], frames.shape[2], frames.shape[4]
    w_three, w_four = (weight3[0], weight4[0])
    c_mid, c_out = w_three.shape[1], w_four.shape[1]
    taps3, taps4 = w_three.reshape(9, c_in, c_mid), w_four.reshape(9, c_mid, c_out)
    size = lax.axis_size("wide")
    ring = Ring(size)
    core = ring.core
    total_frames = count * size * lax.axis_size("narrow")
    def cells_first(field):
        return jnp.transpose(field, (1, 2, 0, 3))

    def frames_first(field):
        return jnp.transpose(field, (2, 0, 1, 3))

    output, act_mine, slope3, field_mine, send = head(
        total_frames, clip_counts, cells_first(frames[0]), w_three, bias3, w_four, bias4,
        cells_first(cotangent[0]),
    )
    small = size <= 8
    chunks = size if small else 1
    lanes4 = 2 if small else 1
    theirs = swap_cores(send)
    delta3, sums = back4(count, send, slope3, taps4)
    sums_theirs = swap_cores(sums)
    delta3_theirs = swap_cores(delta3)
    grads4 = grad(
        62, side, count, lanes4, chunks, size, c_out,
        (after(act_mine, delta3), 0), (theirs, c_out), (send, 0), (theirs, 0),
    )
    def grad_of_3(mine, sums):
        return grad(
            62, side, count, 1, chunks, size, c_mid,
            (mine, 0), (theirs, c_out + c_mid // 2), (delta3, 0), (delta3_theirs, 0), sums,
        )[0]

    if not small:
        grads3 = grad_of_3(field_mine, ())
        biases = lax.psum(sums + sums_theirs, "wide")
        sum3, sum4 = biases[0:1], biases[1:2]
        grad_w4 = collected(grads4[0][0].reshape(9, -1, c_out), core)
        grad_w3 = collected(grads3[0].reshape(9, -1, c_mid), core)
    else:
        half3, half4, quarter = c_in // 2, c_mid // 2, c_mid // 4
        blocks = 9 * quarter // (8 * size)
        x = Lane(grads4[0], ring, 0, half4, blocks)
        y = Lane(grads4[1], ring, quarter, half4, blocks)
        x.step(0)
        y.step(0)
        grads3 = grad_of_3(field_mine, (sums, sums_theirs))
        z = Lane(grads3, ring, 0, half3, 9 * half3 // (8 * size))
        z.held = after(z.held, x.held, y.held)
        x.held, y.held = after(x.held, z.held), after(y.held, z.held)
        grad_w4 = grad_w3 = None
        shape3, shape4 = (9, c_in, c_mid), (9, c_mid, c_out)
        last = 2 * (size - 1) - 1
        for number in range(last + 1):
            if number in (last - 4, last - 1):
                (grad_w3,) = lay_lanes([(z, 0)], [grad_w3], [shape3])
            if number in (last - 3, last):
                z.held = after(z.held, grad_w3)
            if number in (last - 3, last - 1):
                (grad_w4,) = lay_lanes([(y, 0)], [grad_w4], [shape4])
            if number in (last - 2, last):
                y.held = after(y.held, grad_w4)
                (grad_w4,) = lay_lanes([(x, 0)], [grad_w4], [shape4])
            if number in (last - 1, last):
                x.held = after(x.held, grad_w4)
            z.step(number)
            if number > 0:
                y.step(number)
                x.step(number)
            if number == size - 1:
                sum3, sum4 = tally(z.passed)
            if number == size:
                x.held = after(x.held, sum3)
            if number == 1:
                field_grad = back3(side, count, [after(delta3, z.held)], taps3)
            if number == 3:
                z.held = after(z.held, field_grad)
        grad_w3, grad_w4 = lay_lanes([(z, 0), (x, 1), (y, 1)], [grad_w3, grad_w4], [shape3, shape4])
    if not small:
        field_grad = back3(side, count, [delta3], taps3)
    return (
        frames_first(output)[None],
        frames_first(field_grad)[None],
        grad_w3.reshape(w_three.shape)[None],
        sum3,
        grad_w4.reshape(w_four.shape)[None],
        sum4,
    )


def solution(mesh):
    return jax.shard_map(
        body,
        mesh=mesh,
        in_specs=(
            P("stream", ("wide", "narrow"), None, None, None),
            P("stream", None, None),
            P("stream", None),
            P("stream", None, None),
            P("stream", None),
            P("stream", ("wide", "narrow"), None, None, None),
            P(),
        ),
        out_specs=(
            P("stream", ("wide", "narrow"), None, None, None),
            P("stream", ("wide", "narrow"), None, None, None),
            P("stream", None, None),
            P("stream", None),
            P("stream", None, None),
            P("stream", None),
        ),
        check_vma=False,
    )
```

```python
import functools

import jax
import jax.numpy as jnp
from jax import lax
from jax.experimental import pallas as pl
from jax.experimental.pallas import tpu as pltpu
from jax.sharding import PartitionSpec as P

BF16 = jnp.bfloat16
F32 = jnp.float32
STEP = 16
MIB = 1024 * 1024
HEAD_MIB, BACK4_MIB, BACK3_MIB = 60, 62, 16
HBM = pl.BlockSpec(memory_space=pltpu.HBM)


def own_place(size):
    core, wide = lax.axis_index("narrow"), lax.axis_index("wide")
    half = lax.div(wide, 2)
    return core, jnp.where(lax.rem(wide, 2) == 0, half, size - 1 - half), 1 - 2 * core


def kernel_call(kernel, outs, scratch, mib, flops, *args, aliases={}):
    return pl.pallas_call(
        kernel,
        out_shape=outs,
        in_specs=[HBM] * len(args),
        out_specs=jax.tree.map(lambda _: HBM, outs),
        scratch_shapes=scratch,
        input_output_aliases=aliases,
        compiler_params=pltpu.CompilerParams(vmem_limit_bytes=mib * MIB),
        cost_estimate=pl.CostEstimate(flops=flops, bytes_accessed=8 * MIB, transcendentals=0),
    )(*args)


def spread_block(block, cat_ref, i, count):
    edge, width = block.shape
    here = pl.ds(pl.multiple_of((i + 1) * edge, edge), edge)
    for at, shift in enumerate((count, 0, edge - count)):
        moved = block if shift == 0 else pltpu.roll(block, shift, 0)
        cat_ref[here, at * width : (at + 1) * width] = moved.astype(BF16)


def clear_edges(cat_ref, count):
    edge = count * STEP
    zeros = jnp.zeros((edge, cat_ref.shape[1]), cat_ref.dtype)
    cat_ref[0:edge, :] = zeros
    cat_ref[cat_ref.shape[0] - edge :, :] = zeros


def convolve_into(acc_ref, cat_ref, w_ref, edge):
    rows, width = acc_ref.shape[0], cat_ref.shape[1]
    for r in range(3):
        part = jnp.dot(
            cat_ref[r * edge : r * edge + rows, :],
            w_ref[r * width : (r + 1) * width, :],
            preferred_element_type=F32,
        )
        if r == 0:
            acc_ref[...] = part
        else:
            acc_ref[...] += part


def back_into(acc_ref, cat_ref, w_ref, edge, loads):
    rows, width = acc_ref.shape[0], w_ref.shape[2]
    for r in range(3):
        loads[r].wait()
        for c in range(3):
            part = lax.dot_general(
                cat_ref[(2 - r) * edge : (2 - r) * edge + rows, (2 - c) * width : (3 - c) * width],
                w_ref[3 * r + c],
                (((1,), (1,)), ((), ())),
                preferred_element_type=F32,
            )
            if r + c == 0:
                acc_ref[...] = part
            else:
                acc_ref[...] += part


def silu_slope(value, sigma):
    return sigma * (1.0 + value * (1.0 - sigma))


def head_kernel(
    total, counts_hbm, frames_hbm, w3_hbm, b3_hbm, w4_hbm, b4_hbm, cot_hbm,
    out_hbm, mine_hbm, slope_hbm, delta_hbm, field_mine_hbm, send_hbm,
    counts_ref, frames_ref, w3_ref, b3_ref, w4_ref, b4_ref, cot_ref,
    field_ref, act_ref, acc_ref, slope_ref, delta_ref, short_ref, out_ref, block3_ref, block_ref, cat3_ref, cat4_ref,
    in_sems, out_sems,
):
    sources = (frames_hbm, counts_hbm, w3_hbm, b3_hbm, b4_hbm, w4_hbm, cot_hbm)
    targets = (frames_ref, counts_ref, w3_ref, b3_ref, b4_ref, w4_ref, cot_ref)
    loads = [
        pltpu.make_async_copy(source, target, in_sems.at[at])
        for at, (source, target) in enumerate(zip(sources, targets))
    ]
    for load in loads:
        load.start()
    side, count = frames_ref.shape[0], frames_ref.shape[2]
    edge = count * STEP
    rows = side * edge
    valid = side * count
    videos = counts_ref.shape[0]
    half3, half4 = field_mine_hbm.shape[1], mine_hbm.shape[1]
    c_mid, c_out = slope_ref.shape[1], delta_ref.shape[1]

    block3_ref[...] = jnp.zeros_like(block3_ref)
    block_ref[...] = jnp.zeros_like(block_ref)
    clear_edges(cat3_ref, count)
    clear_edges(cat4_ref, count)
    for load in loads[:2]:
        load.wait()

    def gather(i, _):
        for j in range(side):
            block3_ref[j * count : (j + 1) * count, :] = frames_ref[i, j].astype(F32)
        block = block3_ref[...]
        field_ref[pl.ds(pl.multiple_of(i * edge, edge), edge), :] = block
        spread_block(block, cat3_ref, i, count)
        return 0

    lax.fori_loop(0, side, gather, 0, unroll=True)
    core = lax.axis_index("narrow")
    first = (lax.axis_index("wide") * lax.axis_size("narrow") + core) * count

    def part(at, half, start=0):
        return pl.ds(pl.multiple_of(start + at * half, half), half)

    inner = slice(edge, edge + rows)
    stores = [
        pltpu.make_async_copy(
            cat3_ref.at[inner, part(core, half3, 2 * half3)], field_mine_hbm, out_sems.at[0]
        ),
        pltpu.make_async_copy(
            field_ref.at[:, part(1 - core, half3)], send_hbm.at[:, c_out + half4 :], out_sems.at[1]
        ),
    ]

    def owned(f):
        index = first + f

        def look(v, carry):
            start, found = carry
            end = start + counts_ref[v]
            inside = jnp.logical_and(index >= start, index < end)
            return end, jnp.where(inside, counts_ref[v], found)

        return lax.fori_loop(0, videos, look, (jnp.int32(0), jnp.int32(1)))[1]

    row = lax.broadcasted_iota(jnp.int32, (edge, 1), 0)
    held = jnp.zeros((edge, 1), jnp.int32)
    for f in range(count):
        held = jnp.where(lax.rem(row, count) == f, owned(f), held)
    scale = total / (videos * held.astype(F32))
    for load in loads[2:5]:
        load.wait()
    convolve_into(acc_ref, cat3_ref, w3_ref, edge)
    bias3 = b3_ref[...].astype(F32)

    def silu_rows(i, _):
        here = pl.ds(pl.multiple_of(i * edge, edge), edge)
        pre = acc_ref[here, :] + bias3
        sigma = jax.nn.sigmoid(pre)
        slope_ref[here, :] = silu_slope(pre, sigma)
        act = jnp.where(row < valid, pre * sigma, 0.0).astype(BF16).astype(F32)
        act_ref[here, :] = act
        spread_block(act, cat4_ref, i, count)
        return 0

    lax.fori_loop(0, side, silu_rows, 0, unroll=True)
    stores += [
        pltpu.make_async_copy(
            act_ref.at[:, part(1 - core, half4)], send_hbm.at[:, c_out : c_out + half4], out_sems.at[2]
        ),
        pltpu.make_async_copy(cat4_ref.at[inner, part(core, half4, c_mid)], mine_hbm, out_sems.at[3]),
        pltpu.make_async_copy(slope_ref, slope_hbm, out_sems.at[4]),
    ]
    for store in stores:
        store.start()
    for load in loads[5:]:
        load.wait()
    convolve_into(acc_ref, cat4_ref, w4_ref, edge)
    bias4 = b4_ref[...].astype(F32)

    def last_rows(i, _):
        here = pl.ds(pl.multiple_of(i * edge, edge), edge)
        for j in range(side):
            block_ref[j * count : (j + 1) * count, :] = cot_ref[i, j].astype(F32)
        pre = acc_ref[here, :] + bias4
        sigma = jax.nn.sigmoid(pre)
        delta = (block_ref[...] * scale * silu_slope(pre, sigma)).astype(BF16)
        short_ref[here, :] = delta
        delta_ref[here, :] = delta.astype(F32)
        pltpu.make_async_copy(delta_ref.at[here], send_hbm.at[here, 0:c_out], out_sems.at[5]).start()
        out = pre * sigma
        for j in range(side):
            out_ref[i, j] = out[j * count : (j + 1) * count, :].astype(BF16)
        return 0

    lax.fori_loop(0, side, last_rows, 0, unroll=True)
    late = [
        pltpu.make_async_copy(short_ref, delta_hbm, out_sems.at[6]),
        pltpu.make_async_copy(out_ref, out_hbm, out_sems.at[7]),
    ]
    for store in late:
        store.start()
    stores.append(pltpu.make_async_copy(delta_ref, send_hbm.at[:, 0:c_out], out_sems.at[5]))
    for store in stores + late:
        store.wait()


def head(total, clip_counts, frames, w3, b3, w4, b4, cot):
    side, count, c_in = frames.shape[1:]
    c_mid, c_out = w3.shape[1], w4.shape[1]
    rows = side * count * STEP
    edges = rows + 2 * count * STEP

    def field(width, dtype):
        return jax.ShapeDtypeStruct((rows, width), dtype)

    return kernel_call(
        functools.partial(head_kernel, float(total)),
        (
            jax.ShapeDtypeStruct(cot.shape, BF16),
            field(c_mid // 2, BF16),
            field(c_mid, F32),
            field(c_out, BF16),
            field(c_in // 2, BF16),
            field(c_out + c_mid // 2 + c_in // 2, F32),
        ),
        [
            pltpu.SMEM(clip_counts.shape, jnp.int32),
            pltpu.VMEM(frames.shape, BF16),
            pltpu.VMEM(w3.shape, BF16),
            pltpu.VMEM(b3.shape, BF16),
            pltpu.VMEM(w4.shape, BF16),
            pltpu.VMEM(b4.shape, BF16),
            pltpu.VMEM(cot.shape, BF16),
            pltpu.VMEM((rows, c_in), F32),
            pltpu.VMEM((rows, c_mid), F32),
            pltpu.VMEM((rows, c_mid), F32),
            pltpu.VMEM((rows, c_mid), F32),
            pltpu.VMEM((rows, c_out), F32),
            pltpu.VMEM((rows, c_out), BF16),
            pltpu.VMEM(cot.shape, BF16),
            pltpu.VMEM((count * STEP, c_in), F32),
            pltpu.VMEM((count * STEP, c_out), F32),
            pltpu.VMEM((edges, 3 * c_in), BF16),
            pltpu.VMEM((edges, 3 * c_mid), BF16),
            pltpu.SemaphoreType.DMA((7,)),
            pltpu.SemaphoreType.DMA((8,)),
        ],
        HEAD_MIB,
        2 * rows * 9 * c_mid * (c_in + c_out),
        clip_counts, frames, w3, b3, w4, b4, cot,
    )


def spread_delta(side, count, delta_ref, cat_ref):
    edge = count * STEP
    clear_edges(cat_ref, count)

    def rows_of(i, _):
        block = delta_ref[pl.ds(pl.multiple_of(i * edge, edge), edge), :]
        spread_block(block.astype(F32), cat_ref, i, count)
        return 0

    return lambda: lax.fori_loop(0, side, rows_of, 0, unroll=True)


def back4_kernel(
    count, delta_hbm, slope_hbm, w_hbm, out_hbm, short_hbm, sums_hbm,
    delta_ref, slope_ref, w_ref, cat_ref, acc_ref, out_ref, short_ref, sums_ref, sems,
):
    edge = count * STEP
    rows = out_ref.shape[0]
    side = rows // edge
    load = pltpu.make_async_copy(delta_hbm, delta_ref, sems.at[0])
    load_slope = pltpu.make_async_copy(slope_hbm, slope_ref, sems.at[1])
    load_w = [
        pltpu.make_async_copy(w_hbm.at[3 * r : 3 * r + 3], w_ref.at[3 * r : 3 * r + 3], sems.at[2 + r])
        for r in range(3)
    ]
    for copy in [load] + load_w + [load_slope]:
        copy.start()
    spread = spread_delta(side, count, delta_ref, cat_ref)
    load.wait()
    spread()
    back_into(acc_ref, cat_ref, w_ref, edge, load_w)
    load_slope.wait()
    valid = lax.broadcasted_iota(jnp.int32, (edge, 1), 0) < side * count

    def rows_of(i, carry):
        here = pl.ds(pl.multiple_of(i * edge, edge), edge)
        delta = jnp.where(valid, acc_ref[here, :] * slope_ref[here, :], 0.0).astype(BF16)
        short_ref[here, :] = delta
        long = delta.astype(F32)
        out_ref[here, :] = long
        sum3, sum4 = carry
        return (
            sum3 + jnp.sum(long, 0, keepdims=True),
            sum4 + jnp.sum(delta_ref[here, :].astype(F32), 0, keepdims=True),
        )

    def store(i):
        here = pl.ds(pl.multiple_of(i * edge, edge), edge)
        return pltpu.make_async_copy(out_ref.at[here], out_hbm.at[here], sems.at[5])

    def stored_rows(i, carry):
        carry = rows_of(i, carry)
        store(i).start()
        return carry

    nothing = (jnp.zeros((1, out_ref.shape[1]), F32), jnp.zeros((1, delta_ref.shape[1]), F32))
    sum3, sum4 = rows_of(side - 1, lax.fori_loop(0, side - 1, stored_rows, nothing, unroll=True))
    sums_ref[0:1, :], sums_ref[1:2, :] = sum3, sum4
    spare = (side - 1) * edge + (side + 1) * count
    out_ref[spare : spare + 2, :] = sums_ref[...]
    store(side - 1).start()
    late = [
        pltpu.make_async_copy(short_ref, short_hbm, sems.at[6]),
        pltpu.make_async_copy(sums_ref, sums_hbm, sems.at[7]),
    ]
    for copy in late:
        copy.start()
    for copy in late + [pltpu.make_async_copy(out_ref, out_hbm, sems.at[5])]:
        copy.wait()


def back4(count, delta, slope, w):
    rows, width = delta.shape
    taps, c_mid, _ = w.shape
    return kernel_call(
        functools.partial(back4_kernel, count),
        (
            jax.ShapeDtypeStruct((rows, c_mid), F32),
            jax.ShapeDtypeStruct((rows, c_mid), BF16),
            jax.ShapeDtypeStruct((2, width), F32),
        ),
        [
            pltpu.VMEM((rows, width), BF16),
            pltpu.VMEM((rows, c_mid), F32),
            pltpu.VMEM(w.shape, BF16),
            pltpu.VMEM((rows + 2 * count * STEP, 3 * width), BF16),
            pltpu.VMEM((rows, c_mid), F32),
            pltpu.VMEM((rows, c_mid), F32),
            pltpu.VMEM((rows, c_mid), BF16),
            pltpu.VMEM((2, width), F32),
            pltpu.SemaphoreType.DMA((8,)),
        ],
        BACK4_MIB,
        2 * rows * c_mid * width * taps,
        delta, slope, w,
    )


def back3_kernel(count, delta_hbm, w_hbm, out_hbm, delta_ref, w_ref, cat_ref, acc_ref, out_ref, sems):
    edge = count * STEP
    side = out_ref.shape[0]
    load = pltpu.make_async_copy(delta_hbm, delta_ref, sems.at[0])
    load_w = [
        pltpu.make_async_copy(w_hbm.at[3 * r : 3 * r + 3], w_ref.at[3 * r : 3 * r + 3], sems.at[1 + r])
        for r in range(3)
    ]
    for copy in [load] + load_w:
        copy.start()
    spread = spread_delta(side, count, delta_ref, cat_ref)
    load.wait()
    spread()
    back_into(acc_ref, cat_ref, w_ref, edge, load_w)

    def rows_of(i, _):
        block = acc_ref[pl.ds(pl.multiple_of(i * edge, edge), edge), :]
        for j in range(side):
            out_ref[i, j] = block[j * count : (j + 1) * count, :].astype(BF16)
        return 0

    lax.fori_loop(0, side, rows_of, 0, unroll=True)
    store = pltpu.make_async_copy(out_ref, out_hbm, sems.at[4])
    store.start()
    store.wait()


def back3(side, count, delta, w):
    rows, width = delta.shape
    taps, c_in, _ = w.shape
    return kernel_call(
        functools.partial(back3_kernel, count),
        jax.ShapeDtypeStruct((side, side, count, c_in), BF16),
        [
            pltpu.VMEM((rows, width), BF16),
            pltpu.VMEM(w.shape, BF16),
            pltpu.VMEM((rows + 2 * count * STEP, 3 * width), BF16),
            pltpu.VMEM((rows, c_in), F32),
            pltpu.VMEM((side, side, count, c_in), BF16),
            pltpu.SemaphoreType.DMA((5,)),
        ],
        BACK3_MIB,
        2 * rows * c_in * width * taps,
        delta, w,
    )


def grad_kernel(count, side, lanes, chunks, size, places, tail, *refs):
    sums_hbm, refs = refs[4 : 4 + tail], refs[:4] + refs[4 + tail :]
    outs, (*targets, turned_ref, both_ref, acc_ref, sums_ref, in_sems, out_sems) = (
        refs[4 : 4 + 2 * lanes], refs[4 + 2 * lanes :],
    )
    mine_ref, theirs_ref, other_ref = targets
    _, spot, way = own_place(size)
    edge = count * STEP
    wide = 2 * edge
    k = mine_ref.shape[1]
    groups = (0, side // 3, 2 * side // 3, side)
    loads = []
    for group in range(3):
        steps = slice(groups[group], groups[group + 1])
        rows = slice(groups[group] * edge, groups[group + 1] * edge)
        loads.append([])
        for at, source in enumerate(refs[:4]):
            if at == 2:
                target = both_ref.at[steps, 0:edge]
                source = source.at[steps]
            else:
                target = targets[min(at, 2)]
                source = source.at[rows, places[at] : places[at] + target.shape[1]]
                target = target.at[rows]
            copy = pltpu.make_async_copy(source, target, in_sems.at[at, group])
            copy.start()
            loads[-1].append(copy)
    extra = [pltpu.make_async_copy(source, sums_ref, in_sems.at[4, 0]) for source in sums_hbm]
    for load in extra:
        load.start()
    turned_ref[:, 0:wide] = jnp.zeros((3 * k, wide), BF16)
    turned_ref[:, (side + 1) * wide :] = jnp.zeros((3 * k, wide), BF16)

    def turn(i, carry):
        here = pl.ds(pl.multiple_of(i * edge, edge), edge)
        there = pl.ds(pl.multiple_of((i + 1) * wide, wide), wide)
        turned = jnp.concatenate([mine_ref[here, :].astype(F32), theirs_ref[here, :]], 0).T
        for c, shift in enumerate((count, 0, wide - count)):
            moved = turned if shift == 0 else pltpu.roll(turned, shift, 1)
            turned_ref[c * k : (c + 1) * k, there] = moved.astype(BF16)
        both_ref[i, edge:wide, :] = other_ref[here, :].astype(BF16)
        return carry

    for group in range(3):
        for load in loads[group]:
            load.wait()
        lax.fori_loop(groups[group], groups[group + 1], turn, 0, unroll=True)
    blocks = 3 * k // (8 * lanes * chunks)
    if tail:
        for load in extra:
            load.wait()
        acc_ref[0, :, 3 * blocks] = jnp.zeros((chunks,) + acc_ref.shape[3:], F32)
        spare = (side - 1) * edge + (side + 1) * count
        acc_ref[0, 0, 3 * blocks, 0:2, :] = sums_ref[...] + other_ref[spare : spare + 2, :]
    stores = []
    for r in range(3):
        part = jnp.dot(
            turned_ref[:, r * wide : (r + side) * wide],
            both_ref[...].reshape(side * wide, both_ref.shape[2]),
            preferred_element_type=F32,
        )
        part = part.reshape((3, lanes, chunks, blocks // 3, 8, part.shape[1]))
        for chunk in range(chunks):
            at = lax.rem(way * (spot - chunk) + 2 * size - 1, size) if chunks > 1 else 0
            for lane in range(lanes):
                piece = part[:, lane, chunk].reshape((blocks,) + acc_ref.shape[3:])
                acc_ref[lane, at, r * blocks : (r + 1) * blocks] = piece
        here = slice(r * blocks, (r + 1) * blocks if r < 2 else acc_ref.shape[2])
        for lane in range(lanes):
            first, others = outs[2 * lane : 2 * lane + 2]
            pairs = [(acc_ref.at[lane, 0, here], first.at[here])]
            if chunks > 1:
                pairs.append((acc_ref.at[lane, 1:, here], others.at[:, here]))
            for source, target in pairs:
                copy = pltpu.make_async_copy(source, target, out_sems.at[len(stores)])
                copy.start()
                stores.append(copy)
    for store in stores:
        store.wait()


def grad(mib, side, count, lanes, chunks, size, o, mine, theirs, delta, other, sums=()):
    arrays, places = zip(mine, theirs, delta, other)
    rows, k = arrays[0].shape
    arrays = arrays[:2] + (arrays[2].reshape(side, count * STEP, o),) + arrays[3:]
    blocks = 9 * k // (8 * lanes * chunks) + (1 if sums else 0)
    first = jax.ShapeDtypeStruct((blocks, 8, o), F32)
    others = jax.ShapeDtypeStruct((max(chunks - 1, 1), blocks, 8, o), F32)
    results = kernel_call(
        functools.partial(grad_kernel, count, side, lanes, chunks, size, places, bool(sums)),
        (first, others) * lanes,
        [
            pltpu.VMEM((rows, k), BF16),
            pltpu.VMEM((rows, k), F32),
            pltpu.VMEM((rows, o), F32),
            pltpu.VMEM((3 * k, 2 * count * STEP * (side + 2)), BF16),
            pltpu.VMEM((side, 2 * count * STEP, o), BF16),
            pltpu.VMEM((lanes, chunks, blocks, 8, o), F32),
            pltpu.VMEM((2, o), F32),
            pltpu.SemaphoreType.DMA((5, 3)),
            pltpu.SemaphoreType.DMA((6 * lanes,)),
        ],
        mib,
        2 * 2 * rows * 9 * k * o,
        *arrays, *sums,
    )
    return [(results[2 * lane], results[2 * lane + 1]) for lane in range(lanes)]


def lay_kernel(layout, size, inputs, *refs):
    outs, sems = refs[inputs:-1], refs[-1]
    core, spot, way = own_place(size)
    copies = []
    for at, (out, low, stride, back, own) in enumerate(layout):
        rows = refs[at].shape[1]
        chunk = lax.rem(spot - way * (back if own else -back) + 2 * size, size)
        start = low + (core if own else 1 - core) * stride + chunk * rows
        there = outs[out].at[:, pl.ds(pl.multiple_of(start, rows), rows), :]
        copies.append(pltpu.make_async_copy(refs[at], there, sems.at[at]))
    for copy in copies:
        copy.start()
    for copy in copies:
        copy.wait()


def lay(size, pieces, layout, results, shapes):
    kept = [at for at, result in enumerate(results) if result is not None]
    inputs = len(pieces) + len(kept)
    return kernel_call(
        functools.partial(lay_kernel, tuple(layout), size, inputs),
        tuple(jax.ShapeDtypeStruct(shape, F32) for shape in shapes),
        [pltpu.SemaphoreType.DMA((len(pieces),))],
        1,
        0,
        *pieces, *[results[at] for at in kept],
        aliases={len(pieces) + at: out for at, out in enumerate(kept)},
    )


def tally_kernel(size, *refs):
    pieces, (first_hbm, second_hbm, all_ref, total_ref, in_sems, out_sems) = refs[:size], refs[size:]
    _, spot, way = own_place(size)
    loads = []
    for back, piece in enumerate(pieces):
        chunk = lax.rem(spot - way * back + 2 * size, size)
        loads.append(pltpu.make_async_copy(piece.at[piece.shape[0] - 1], all_ref.at[chunk], in_sems.at[back]))
        loads[-1].start()
    for load in loads:
        load.wait()
    total = all_ref[0]
    for chip in range(1, size):
        total = total + all_ref[chip]
    total_ref[0] = total[0:1]
    total_ref[1] = total[1:2]
    stores = [
        pltpu.make_async_copy(total_ref.at[at], out, out_sems.at[at])
        for at, out in enumerate((first_hbm, second_hbm))
    ]
    for store in stores:
        store.start()
    for store in stores:
        store.wait()


def tally(pieces):
    size, width = len(pieces), pieces[0].shape[2]
    out = jax.ShapeDtypeStruct((1, width), F32)
    return kernel_call(
        functools.partial(tally_kernel, size),
        (out, out),
        [
            pltpu.VMEM((size, 8, width), F32),
            pltpu.VMEM((2, 1, width), F32),
            pltpu.SemaphoreType.DMA((size,)),
            pltpu.SemaphoreType.DMA((2,)),
        ],
        2,
        0,
        *pieces,
    )


def swap_cores(value):
    return lax.ppermute(value, "narrow", [(0, 1), (1, 0)])


def pick(array, index, axis=0):
    return lax.dynamic_index_in_dim(array, index, axis, keepdims=False)


class Ring:
    def __init__(self, size, zero):
        self.size = size
        order = list(range(0, size, 2)) + list(range(size - 1, 0, -2))
        self.pairs = []
        for core, way in ((0, 1), (1, -1)):
            for i in range(size):
                self.pairs.append((2 * order[i] + core, 2 * order[(i + way) % size] + core))
        wide = lax.axis_index("wide")
        self.core = lax.axis_index("narrow")
        half = wide // 2
        self.place = jnp.where(wide % 2 == 0, half, size - 1 - half)
        self.way = 1 - 2 * self.core
        self.zero = zero

    def send(self, value):
        return lax.ppermute(value, ("wide", "narrow"), self.pairs)

    def chunk(self, back):
        return lax.rem(self.place - self.way * back + 2 * self.size, self.size)


def collected(grad, core):
    taps, rows, width = grad.shape
    share = lax.psum_scatter(grad.reshape(-1, width), "wide", scatter_dimension=0, tiled=True)
    mine = lax.all_gather(share, "wide", axis=0, tiled=True).reshape(grad.shape)
    theirs = swap_cores(mine)
    lower, upper = jnp.where(core == 0, mine, theirs), jnp.where(core == 0, theirs, mine)
    return jnp.concatenate([lower, upper], 1)


class Lane:
    def __init__(self, parts, ring, low, stride, blocks):
        self.ring, self.low, self.stride, self.blocks = ring, low, stride, blocks
        self.held, self.parts = parts
        self.passed = [self.held]
        self.pieces, self.lows = [], []

    def keep(self, back):
        for piece, own in ((self.held, True), (swap_cores(self.held), False)):
            self.pieces.append(piece.reshape(9, -1, piece.shape[-1]))
            self.lows.append((self.low, self.stride, back, own))

    def step(self, number):
        last = self.ring.size - 1
        if number == last:
            self.keep(0)
        got = self.got = self.ring.send(self.held)
        if number < last:
            self.passed.append(got)
            if number < last - 1:
                self.held = got + self.parts[number]
            else:
                self.held = got[: self.blocks] + self.parts[number, : self.blocks]
        else:
            self.held = got + self.ring.zero
            self.keep(number - last + 1)


def lay_lanes(lanes, results, shapes):
    pieces, layout = [], []
    for lane, at in lanes:
        pieces += lane.pieces
        layout += [(at,) + low for low in lane.lows]
        size, lane.pieces, lane.lows = lane.ring.size, [], []
    return lay(size, pieces, layout, results, shapes)


def after(value, *others):
    return lax.optimization_barrier((value,) + others)[0]


def body(frames, weight3, bias3, weight4, bias4, cotangent, clip_counts):
    count, side, c_in = frames.shape[1], frames.shape[2], frames.shape[4]
    w_three, w_four = (weight3[0], weight4[0])
    c_mid, c_out = w_three.shape[1], w_four.shape[1]
    taps3, taps4 = w_three.reshape(9, c_in, c_mid), w_four.reshape(9, c_mid, c_out)
    size = lax.axis_size("wide")
    ring = Ring(size, jnp.minimum(clip_counts[0], 0).astype(F32))
    core = ring.core
    total_frames = count * size * lax.axis_size("narrow")
    def cells_first(field):
        return jnp.transpose(field, (1, 2, 0, 3))

    def frames_first(field):
        return jnp.transpose(field, (2, 0, 1, 3))

    output, act_mine, slope3, delta4, field_mine, send = head(
        total_frames, clip_counts, cells_first(frames[0]), w_three, bias3, w_four, bias4,
        cells_first(cotangent[0]),
    )
    small = size <= 8
    chunks = size if small else 1
    lanes4 = 2 if small else 1
    theirs = swap_cores(send)
    delta3_sums, delta3, sums = back4(count, delta4, slope3, taps4)
    delta3_theirs = swap_cores(delta3_sums)
    grads4 = grad(
        62, side, count, lanes4, chunks, size, c_out,
        (after(act_mine, delta3), 0), (theirs, c_out), (delta4, 0), (theirs, 0),
    )
    def grad_of_3(mine, sums):
        return grad(
            24, side, count, 1, chunks, size, c_mid,
            (mine, 0), (theirs, c_out + c_mid // 2), (delta3, 0), (delta3_theirs, 0), sums,
        )[0]

    if not small:
        grads3 = grad_of_3(field_mine, ())
        biases = lax.psum(sums, ("wide", "narrow"))
        sum3, sum4 = biases[0:1], biases[1:2]
        grad_w4 = collected(grads4[0][0].reshape(9, -1, c_out), core)
        grad_w3 = collected(grads3[0].reshape(9, -1, c_mid), core)
    else:
        half3, half4, quarter = c_in // 2, c_mid // 2, c_mid // 4
        blocks = 9 * quarter // (8 * size)
        x = Lane(grads4[0], ring, 0, half4, blocks)
        y = Lane(grads4[1], ring, quarter, half4, blocks)
        x.step(0)
        y.step(0)
        grads3 = grad_of_3(field_mine, (sums,))
        z = Lane(grads3, ring, 0, half3, 9 * half3 // (8 * size))
        z.held = after(z.held, x.got, y.got)
        x.held, y.held = after(x.held, z.held), after(y.held, z.held)
        grad_w4 = grad_w3 = None
        shape3, shape4 = (9, c_in, c_mid), (9, c_mid, c_out)
        last = 2 * (size - 1) - 1
        for number in range(last + 1):
            if number in (last - 4, last - 1):
                (grad_w3,) = lay_lanes([(z, 0)], [grad_w3], [shape3])
            if number in (last - 3, last):
                z.held = after(z.held, grad_w3)
            if number in (last - 3, last - 1):
                (grad_w4,) = lay_lanes([(y, 0)], [grad_w4], [shape4])
            if number in (last - 2, last):
                y.held = after(y.held, grad_w4)
                (grad_w4,) = lay_lanes([(x, 0)], [grad_w4], [shape4])
            if number in (last - 1, last):
                x.held = after(x.held, grad_w4)
            z.step(number)
            if number > 0:
                y.step(number)
                x.step(number)
            if number == size - 1:
                sum3, sum4 = tally(z.passed)
            if number == size:
                x.held = after(x.held, sum3)
            if number == 1:
                field_grad = back3(side, count, after(delta3, z.held), taps3)
            if number == 3:
                z.held = after(z.held, field_grad)
        grad_w3, grad_w4 = lay_lanes([(z, 0), (y, 1)], [grad_w3, grad_w4], [shape3, shape4])
        (grad_w4,) = lay_lanes([(x, 0)], [grad_w4], [shape4])
    if not small:
        field_grad = back3(side, count, delta3, taps3)
    return (
        frames_first(output)[None],
        frames_first(field_grad)[None],
        grad_w3.reshape(w_three.shape)[None],
        sum3,
        grad_w4.reshape(w_four.shape)[None],
        sum4,
    )


def solution(mesh):
    return jax.shard_map(
        body,
        mesh=mesh,
        in_specs=(
            P("stream", ("wide", "narrow"), None, None, None),
            P("stream", None, None),
            P("stream", None),
            P("stream", None, None),
            P("stream", None),
            P("stream", ("wide", "narrow"), None, None, None),
            P(),
        ),
        out_specs=(
            P("stream", ("wide", "narrow"), None, None, None),
            P("stream", ("wide", "narrow"), None, None, None),
            P("stream", None, None),
            P("stream", None),
            P("stream", None, None),
            P("stream", None),
        ),
        check_vma=False,
    )
```

```python
import functools

import jax
import jax.numpy as jnp
from jax import lax
from jax.experimental import pallas as pl
from jax.experimental.pallas import tpu as pltpu
from jax.sharding import PartitionSpec as P

BF16 = jnp.bfloat16
F32 = jnp.float32
STEP = 16
MIB = 1024 * 1024
HEAD_MIB, BACK4_MIB, BACK3_MIB = 60, 62, 16
HBM = pl.BlockSpec(memory_space=pltpu.HBM)


def own_place(size):
    core, wide = lax.axis_index("narrow"), lax.axis_index("wide")
    half = lax.div(wide, 2)
    return core, jnp.where(lax.rem(wide, 2) == 0, half, size - 1 - half), 1 - 2 * core


def kernel_call(kernel, outs, scratch, mib, flops, *args, aliases={}):
    return pl.pallas_call(
        kernel,
        out_shape=outs,
        in_specs=[HBM] * len(args),
        out_specs=jax.tree.map(lambda _: HBM, outs),
        scratch_shapes=scratch,
        input_output_aliases=aliases,
        compiler_params=pltpu.CompilerParams(vmem_limit_bytes=mib * MIB),
        cost_estimate=pl.CostEstimate(flops=flops, bytes_accessed=8 * MIB, transcendentals=0),
    )(*args)


def spread_block(block, cat_ref, i, count):
    edge, width = block.shape
    here = slice((i + 1) * edge, (i + 2) * edge)
    for at, shift in enumerate((count, 0, edge - count)):
        moved = block if shift == 0 else pltpu.roll(block, shift, 0)
        cat_ref[here, at * width : (at + 1) * width] = moved.astype(BF16)


def clear_edges(cat_ref, count):
    edge = count * STEP
    zeros = jnp.zeros((edge, cat_ref.shape[1]), cat_ref.dtype)
    cat_ref[0:edge, :] = zeros
    cat_ref[cat_ref.shape[0] - edge :, :] = zeros


def convolve_into(acc_ref, cat_ref, w_ref, edge):
    rows, width = acc_ref.shape[0], cat_ref.shape[1]
    for r in range(3):
        part = jnp.dot(
            cat_ref[r * edge : r * edge + rows, :],
            w_ref[r * width : (r + 1) * width, :],
            preferred_element_type=F32,
        )
        if r == 0:
            acc_ref[...] = part
        else:
            acc_ref[...] += part


def back_into(acc_ref, cat_ref, w_ref, edge, loads):
    rows, width = acc_ref.shape[0], w_ref.shape[2]
    for r in range(3):
        loads[r].wait()
        for c in range(3):
            part = lax.dot_general(
                cat_ref[(2 - r) * edge : (2 - r) * edge + rows, (2 - c) * width : (3 - c) * width],
                w_ref[3 * r + c],
                (((1,), (1,)), ((), ())),
                preferred_element_type=F32,
            )
            if r + c == 0:
                acc_ref[...] = part
            else:
                acc_ref[...] += part


def silu_slope(value, sigma):
    return sigma * (1.0 + value * (1.0 - sigma))


def head_kernel(
    total, counts_hbm, frames_hbm, w3_hbm, b3_hbm, w4_hbm, b4_hbm, cot_hbm,
    out_hbm, mine_hbm, slope_hbm, delta_hbm, field_mine_hbm, send_hbm,
    counts_ref, frames_ref, w3_ref, b3_ref, w4_ref, b4_ref, cot_ref,
    field_ref, act_ref, acc_ref, slope_ref, delta_ref, short_ref, out_ref, block3_ref, block_ref, cat3_ref, cat4_ref,
    in_sems, out_sems,
):
    sources = (frames_hbm, counts_hbm, w3_hbm, b3_hbm, b4_hbm, w4_hbm, cot_hbm)
    targets = (frames_ref, counts_ref, w3_ref, b3_ref, b4_ref, w4_ref, cot_ref)
    loads = [
        pltpu.make_async_copy(source, target, in_sems.at[at])
        for at, (source, target) in enumerate(zip(sources, targets))
    ]
    for load in loads:
        load.start()
    side, count = frames_ref.shape[0], frames_ref.shape[2]
    edge = count * STEP
    rows = side * edge
    valid = side * count
    videos = counts_ref.shape[0]
    half3, half4 = field_mine_hbm.shape[1], mine_hbm.shape[1]
    c_mid, c_out = slope_ref.shape[1], delta_ref.shape[1]

    block3_ref[...] = jnp.zeros_like(block3_ref)
    block_ref[...] = jnp.zeros_like(block_ref)
    clear_edges(cat3_ref, count)
    clear_edges(cat4_ref, count)
    for load in loads[:2]:
        load.wait()

    def gather(i):
        for j in range(side):
            block3_ref[j * count : (j + 1) * count, :] = frames_ref[i, j].astype(F32)
        block = block3_ref[...]
        field_ref[slice(i * edge, (i + 1) * edge), :] = block
        spread_block(block, cat3_ref, i, count)

    for i in range(side):
        gather(i)
    core = lax.axis_index("narrow")
    first = (lax.axis_index("wide") * lax.axis_size("narrow") + core) * count

    def part(at, half, start=0):
        return pl.ds(pl.multiple_of(start + at * half, half), half)

    inner = slice(edge, edge + rows)
    stores = [
        pltpu.make_async_copy(
            cat3_ref.at[inner, part(core, half3, 2 * half3)], field_mine_hbm, out_sems.at[0, 0]
        ),
        pltpu.make_async_copy(
            field_ref.at[:, part(1 - core, half3)], send_hbm.at[:, c_out + half4 :], out_sems.at[1, 0]
        ),
    ]

    def owned(f):
        index = first + f

        def look(v, carry):
            start, found = carry
            end = start + counts_ref[v]
            inside = jnp.logical_and(index >= start, index < end)
            return end, jnp.where(inside, counts_ref[v], found)

        return lax.fori_loop(0, videos, look, (jnp.int32(0), jnp.int32(1)))[1]

    row = lax.broadcasted_iota(jnp.int32, (edge, 1), 0)
    held = jnp.zeros((edge, 1), jnp.int32)
    for f in range(count):
        held = jnp.where(lax.rem(row, count) == f, owned(f), held)
    scale = total / (videos * held.astype(F32))
    for load in loads[2:5]:
        load.wait()
    convolve_into(acc_ref, cat3_ref, w3_ref, edge)
    bias3 = b3_ref[...].astype(F32)

    def silu_rows(i):
        here = slice(i * edge, (i + 1) * edge)
        pre = acc_ref[here, :] + bias3
        sigma = jax.nn.sigmoid(pre)
        slope_ref[here, :] = silu_slope(pre, sigma)
        act = jnp.where(row < valid, pre * sigma, 0.0).astype(BF16).astype(F32)
        act_ref[here, :] = act
        spread_block(act, cat4_ref, i, count)

    for i in range(side):
        silu_rows(i)
    stores += [
        pltpu.make_async_copy(
            act_ref.at[:, part(1 - core, half4)], send_hbm.at[:, c_out : c_out + half4], out_sems.at[2, 0]
        ),
        pltpu.make_async_copy(cat4_ref.at[inner, part(core, half4, c_mid)], mine_hbm, out_sems.at[3, 0]),
        pltpu.make_async_copy(slope_ref, slope_hbm, out_sems.at[4, 0]),
    ]
    for store in stores:
        store.start()
    for load in loads[5:]:
        load.wait()
    convolve_into(acc_ref, cat4_ref, w4_ref, edge)
    bias4 = b4_ref[...].astype(F32)

    def last_rows(i):
        here = slice(i * edge, (i + 1) * edge)
        for j in range(side):
            block_ref[j * count : (j + 1) * count, :] = cot_ref[i, j].astype(F32)
        pre = acc_ref[here, :] + bias4
        sigma = jax.nn.sigmoid(pre)
        delta = (block_ref[...] * scale * silu_slope(pre, sigma)).astype(BF16)
        short_ref[here, :] = delta
        delta_ref[here, :] = delta.astype(F32)
        out = pre * sigma
        for j in range(side):
            out_ref[i, j] = out[j * count : (j + 1) * count, :].astype(BF16)

    parts = [side * at // 4 for at in range(5)]
    for at in range(4):
        for i in range(parts[at], parts[at + 1]):
            last_rows(i)
        steps = slice(parts[at], parts[at + 1])
        here = slice(parts[at] * edge, parts[at + 1] * edge)
        late = [
            pltpu.make_async_copy(delta_ref.at[here], send_hbm.at[here, 0:c_out], out_sems.at[5, at]),
            pltpu.make_async_copy(short_ref.at[here], delta_hbm.at[here], out_sems.at[6, at]),
            pltpu.make_async_copy(out_ref.at[steps], out_hbm.at[steps], out_sems.at[7, at]),
        ]
        for store in late:
            store.start()
        stores += late
    for store in stores:
        store.wait()


def head(total, clip_counts, frames, w3, b3, w4, b4, cot):
    side, count, c_in = frames.shape[1:]
    c_mid, c_out = w3.shape[1], w4.shape[1]
    rows = side * count * STEP
    edges = rows + 2 * count * STEP

    def field(width, dtype):
        return jax.ShapeDtypeStruct((rows, width), dtype)

    return kernel_call(
        functools.partial(head_kernel, float(total)),
        (
            jax.ShapeDtypeStruct(cot.shape, BF16),
            field(c_mid // 2, BF16),
            field(c_mid, F32),
            field(c_out, BF16),
            field(c_in // 2, BF16),
            field(c_out + c_mid // 2 + c_in // 2, F32),
        ),
        [
            pltpu.SMEM(clip_counts.shape, jnp.int32),
            pltpu.VMEM(frames.shape, BF16),
            pltpu.VMEM(w3.shape, BF16),
            pltpu.VMEM(b3.shape, BF16),
            pltpu.VMEM(w4.shape, BF16),
            pltpu.VMEM(b4.shape, BF16),
            pltpu.VMEM(cot.shape, BF16),
            pltpu.VMEM((rows, c_in), F32),
            pltpu.VMEM((rows, c_mid), F32),
            pltpu.VMEM((rows, c_mid), F32),
            pltpu.VMEM((rows, c_mid), F32),
            pltpu.VMEM((rows, c_out), F32),
            pltpu.VMEM((rows, c_out), BF16),
            pltpu.VMEM(cot.shape, BF16),
            pltpu.VMEM((count * STEP, c_in), F32),
            pltpu.VMEM((count * STEP, c_out), F32),
            pltpu.VMEM((edges, 3 * c_in), BF16),
            pltpu.VMEM((edges, 3 * c_mid), BF16),
            pltpu.SemaphoreType.DMA((7,)),
            pltpu.SemaphoreType.DMA((8, 4)),
        ],
        HEAD_MIB,
        2 * rows * 9 * c_mid * (c_in + c_out),
        clip_counts, frames, w3, b3, w4, b4, cot,
    )


def spread_delta(side, count, delta_ref, cat_ref):
    edge = count * STEP
    clear_edges(cat_ref, count)

    def spread():
        for i in range(side):
            block = delta_ref[i * edge : (i + 1) * edge, :]
            spread_block(block.astype(F32), cat_ref, i, count)

    return spread


def back4_kernel(
    count, delta_hbm, slope_hbm, w_hbm, out_hbm, short_hbm, sums_hbm,
    delta_ref, slope_ref, w_ref, cat_ref, acc_ref, out_ref, short_ref, sums_ref, sems,
):
    edge = count * STEP
    rows = out_ref.shape[0]
    side = rows // edge
    load = pltpu.make_async_copy(delta_hbm, delta_ref, sems.at[0])
    load_slope = pltpu.make_async_copy(slope_hbm, slope_ref, sems.at[1])
    load_w = [
        pltpu.make_async_copy(w_hbm.at[3 * r : 3 * r + 3], w_ref.at[3 * r : 3 * r + 3], sems.at[2 + r])
        for r in range(3)
    ]
    for copy in [load] + load_w + [load_slope]:
        copy.start()
    spread = spread_delta(side, count, delta_ref, cat_ref)
    load.wait()
    spread()
    back_into(acc_ref, cat_ref, w_ref, edge, load_w)
    load_slope.wait()
    valid = lax.broadcasted_iota(jnp.int32, (edge, 1), 0) < side * count

    def rows_of(i):
        here = slice(i * edge, (i + 1) * edge)
        delta = jnp.where(valid, acc_ref[here, :] * slope_ref[here, :], 0.0).astype(BF16)
        short_ref[here, :] = delta
        long = delta.astype(F32)
        out_ref[here, :] = long
        return (
            jnp.sum(long, 0, keepdims=True),
            jnp.sum(delta_ref[here, :].astype(F32), 0, keepdims=True),
        )

    sum3, sum4 = rows_of(0)
    stores = []
    parts = [side * at // 4 for at in range(5)]
    for at in range(4):
        for i in range(max(parts[at], 1), parts[at + 1]):
            more3, more4 = rows_of(i)
            sum3, sum4 = sum3 + more3, sum4 + more4
        if at == 3:
            sums_ref[0:1, :], sums_ref[1:2, :] = sum3, sum4
            spare = (side - 1) * edge + (side + 1) * count
            out_ref[spare : spare + 2, :] = sums_ref[...]
        here = slice(parts[at] * edge, parts[at + 1] * edge)
        stores.append(pltpu.make_async_copy(out_ref.at[here], out_hbm.at[here], sems.at[5 + at]))
        stores.append(pltpu.make_async_copy(short_ref.at[here], short_hbm.at[here], sems.at[9 + at]))
        for store in stores[-2:]:
            store.start()
    stores.append(pltpu.make_async_copy(sums_ref, sums_hbm, sems.at[13]))
    stores[-1].start()
    for store in stores:
        store.wait()


def back4(count, delta, slope, w):
    rows, width = delta.shape
    taps, c_mid, _ = w.shape
    return kernel_call(
        functools.partial(back4_kernel, count),
        (
            jax.ShapeDtypeStruct((rows, c_mid), F32),
            jax.ShapeDtypeStruct((rows, c_mid), BF16),
            jax.ShapeDtypeStruct((2, width), F32),
        ),
        [
            pltpu.VMEM((rows, width), BF16),
            pltpu.VMEM((rows, c_mid), F32),
            pltpu.VMEM(w.shape, BF16),
            pltpu.VMEM((rows + 2 * count * STEP, 3 * width), BF16),
            pltpu.VMEM((rows, c_mid), F32),
            pltpu.VMEM((rows, c_mid), F32),
            pltpu.VMEM((rows, c_mid), BF16),
            pltpu.VMEM((2, width), F32),
            pltpu.SemaphoreType.DMA((14,)),
        ],
        BACK4_MIB,
        2 * rows * c_mid * width * taps,
        delta, slope, w,
    )


def back3_kernel(count, delta_hbm, w_hbm, out_hbm, delta_ref, w_ref, cat_ref, acc_ref, out_ref, sems):
    edge = count * STEP
    side = out_ref.shape[0]
    load = pltpu.make_async_copy(delta_hbm, delta_ref, sems.at[0])
    load_w = [
        pltpu.make_async_copy(w_hbm.at[3 * r : 3 * r + 3], w_ref.at[3 * r : 3 * r + 3], sems.at[1 + r])
        for r in range(3)
    ]
    for copy in [load] + load_w:
        copy.start()
    spread = spread_delta(side, count, delta_ref, cat_ref)
    load.wait()
    spread()
    back_into(acc_ref, cat_ref, w_ref, edge, load_w)

    for i in range(side):
        block = acc_ref[i * edge : (i + 1) * edge, :]
        for j in range(side):
            out_ref[i, j] = block[j * count : (j + 1) * count, :].astype(BF16)
    store = pltpu.make_async_copy(out_ref, out_hbm, sems.at[4])
    store.start()
    store.wait()


def back3(side, count, delta, w):
    rows, width = delta.shape
    taps, c_in, _ = w.shape
    return kernel_call(
        functools.partial(back3_kernel, count),
        jax.ShapeDtypeStruct((side, side, count, c_in), BF16),
        [
            pltpu.VMEM((rows, width), BF16),
            pltpu.VMEM(w.shape, BF16),
            pltpu.VMEM((rows + 2 * count * STEP, 3 * width), BF16),
            pltpu.VMEM((rows, c_in), F32),
            pltpu.VMEM((side, side, count, c_in), BF16),
            pltpu.SemaphoreType.DMA((5,)),
        ],
        BACK3_MIB,
        2 * rows * c_in * width * taps,
        delta, w,
    )


def grad_kernel(count, side, lanes, chunks, size, places, tail, *refs):
    sums_hbm, refs = refs[4 : 4 + tail], refs[:4] + refs[4 + tail :]
    outs, (*targets, turned_ref, both_ref, acc_ref, sums_ref, in_sems, out_sems) = (
        refs[4 : 4 + 2 * lanes], refs[4 + 2 * lanes :],
    )
    mine_ref, theirs_ref, other_ref = targets
    _, spot, way = own_place(size)
    edge = count * STEP
    wide = 2 * edge
    k = mine_ref.shape[1]
    groups = (0, side // 3, 2 * side // 3, side)
    loads = []
    for group in range(3):
        steps = slice(groups[group], groups[group + 1])
        rows = slice(groups[group] * edge, groups[group + 1] * edge)
        loads.append([])
        for at, source in enumerate(refs[:4]):
            if at == 2:
                target = both_ref.at[steps, 0:edge]
                source = source.at[steps]
            else:
                target = targets[min(at, 2)]
                source = source.at[rows, places[at] : places[at] + target.shape[1]]
                target = target.at[rows]
            copy = pltpu.make_async_copy(source, target, in_sems.at[at, group])
            copy.start()
            loads[-1].append(copy)
    extra = [pltpu.make_async_copy(source, sums_ref, in_sems.at[4, 0]) for source in sums_hbm]
    for load in extra:
        load.start()
    turned_ref[:, 0:wide] = jnp.zeros((3 * k, wide), BF16)
    turned_ref[:, (side + 1) * wide :] = jnp.zeros((3 * k, wide), BF16)

    def turn(i):
        here = slice(i * edge, (i + 1) * edge)
        there = slice((i + 1) * wide, (i + 2) * wide)
        turned = jnp.concatenate([mine_ref[here, :].astype(F32), theirs_ref[here, :]], 0).T
        for c, shift in enumerate((count, 0, wide - count)):
            moved = turned if shift == 0 else pltpu.roll(turned, shift, 1)
            turned_ref[c * k : (c + 1) * k, there] = moved.astype(BF16)
        both_ref[i, edge:wide, :] = other_ref[here, :].astype(BF16)

    for group in range(3):
        for load in loads[group]:
            load.wait()
        for i in range(groups[group], groups[group + 1]):
            turn(i)
    blocks = 3 * k // (8 * lanes * chunks)
    if tail:
        for load in extra:
            load.wait()
        acc_ref[0, :, 3 * blocks] = jnp.zeros((chunks,) + acc_ref.shape[3:], F32)
        spare = (side - 1) * edge + (side + 1) * count
        acc_ref[0, 0, 3 * blocks, 0:2, :] = sums_ref[...] + other_ref[spare : spare + 2, :]
    stores = []
    for r in range(3):
        part = jnp.dot(
            turned_ref[:, r * wide : (r + side) * wide],
            both_ref[...].reshape(side * wide, both_ref.shape[2]),
            preferred_element_type=F32,
        )
        part = part.reshape((3, lanes, chunks, blocks // 3, 8, part.shape[1]))
        for chunk in range(chunks):
            at = lax.rem(way * (spot - chunk) + 2 * size - 1, size) if chunks > 1 else 0
            for lane in range(lanes):
                piece = part[:, lane, chunk].reshape((blocks,) + acc_ref.shape[3:])
                acc_ref[lane, at, r * blocks : (r + 1) * blocks] = piece
        here = slice(r * blocks, (r + 1) * blocks if r < 2 else acc_ref.shape[2])
        for lane in range(lanes):
            first, others = outs[2 * lane : 2 * lane + 2]
            pairs = [(acc_ref.at[lane, 0, here], first.at[here])]
            if chunks > 1:
                pairs.append((acc_ref.at[lane, 1:, here], others.at[:, here]))
            for source, target in pairs:
                copy = pltpu.make_async_copy(source, target, out_sems.at[len(stores)])
                copy.start()
                stores.append(copy)
    for store in stores:
        store.wait()


def grad(mib, side, count, lanes, chunks, size, o, mine, theirs, delta, other, sums=()):
    arrays, places = zip(mine, theirs, delta, other)
    rows, k = arrays[0].shape
    arrays = arrays[:2] + (arrays[2].reshape(side, count * STEP, o),) + arrays[3:]
    blocks = 9 * k // (8 * lanes * chunks) + (1 if sums else 0)
    first = jax.ShapeDtypeStruct((blocks, 8, o), F32)
    others = jax.ShapeDtypeStruct((max(chunks - 1, 1), blocks, 8, o), F32)
    results = kernel_call(
        functools.partial(grad_kernel, count, side, lanes, chunks, size, places, bool(sums)),
        (first, others) * lanes,
        [
            pltpu.VMEM((rows, k), BF16),
            pltpu.VMEM((rows, k), F32),
            pltpu.VMEM((rows, o), F32),
            pltpu.VMEM((3 * k, 2 * count * STEP * (side + 2)), BF16),
            pltpu.VMEM((side, 2 * count * STEP, o), BF16),
            pltpu.VMEM((lanes, chunks, blocks, 8, o), F32),
            pltpu.VMEM((2, o), F32),
            pltpu.SemaphoreType.DMA((5, 3)),
            pltpu.SemaphoreType.DMA((6 * lanes,)),
        ],
        mib,
        2 * 2 * rows * 9 * k * o,
        *arrays, *sums,
    )
    return [(results[2 * lane], results[2 * lane + 1]) for lane in range(lanes)]


def lay_kernel(layout, size, inputs, *refs):
    outs, sems = refs[inputs:-1], refs[-1]
    core, spot, way = own_place(size)
    copies = []
    for at, (out, low, stride, back, own) in enumerate(layout):
        rows = refs[at].shape[1]
        chunk = lax.rem(spot - way * (back if own else -back) + 2 * size, size)
        start = low + (core if own else 1 - core) * stride + chunk * rows
        there = outs[out].at[:, pl.ds(pl.multiple_of(start, rows), rows), :]
        copies.append(pltpu.make_async_copy(refs[at], there, sems.at[at]))
    for copy in copies:
        copy.start()
    for copy in copies:
        copy.wait()


def lay(size, pieces, layout, results, shapes):
    kept = [at for at, result in enumerate(results) if result is not None]
    inputs = len(pieces) + len(kept)
    return kernel_call(
        functools.partial(lay_kernel, tuple(layout), size, inputs),
        tuple(jax.ShapeDtypeStruct(shape, F32) for shape in shapes),
        [pltpu.SemaphoreType.DMA((len(pieces),))],
        1,
        0,
        *pieces, *[results[at] for at in kept],
        aliases={len(pieces) + at: out for at, out in enumerate(kept)},
    )


def tally_kernel(size, *refs):
    pieces, (first_hbm, second_hbm, all_ref, total_ref, in_sems, out_sems) = refs[:size], refs[size:]
    _, spot, way = own_place(size)
    loads = []
    for back, piece in enumerate(pieces):
        chunk = lax.rem(spot - way * back + 2 * size, size)
        loads.append(pltpu.make_async_copy(piece.at[piece.shape[0] - 1], all_ref.at[chunk], in_sems.at[back]))
        loads[-1].start()
    for load in loads:
        load.wait()
    total = all_ref[0]
    for chip in range(1, size):
        total = total + all_ref[chip]
    total_ref[0] = total[0:1]
    total_ref[1] = total[1:2]
    stores = [
        pltpu.make_async_copy(total_ref.at[at], out, out_sems.at[at])
        for at, out in enumerate((first_hbm, second_hbm))
    ]
    for store in stores:
        store.start()
    for store in stores:
        store.wait()


def tally(pieces):
    size, width = len(pieces), pieces[0].shape[2]
    out = jax.ShapeDtypeStruct((1, width), F32)
    return kernel_call(
        functools.partial(tally_kernel, size),
        (out, out),
        [
            pltpu.VMEM((size, 8, width), F32),
            pltpu.VMEM((2, 1, width), F32),
            pltpu.SemaphoreType.DMA((size,)),
            pltpu.SemaphoreType.DMA((2,)),
        ],
        2,
        0,
        *pieces,
    )


def swap_cores(value):
    return lax.ppermute(value, "narrow", [(0, 1), (1, 0)])


def pick(array, index, axis=0):
    return lax.dynamic_index_in_dim(array, index, axis, keepdims=False)


class Ring:
    def __init__(self, size):
        self.size = size
        order = list(range(0, size, 2)) + list(range(size - 1, 0, -2))
        self.pairs = []
        for core, way in ((0, 1), (1, -1)):
            for i in range(size):
                self.pairs.append((2 * order[i] + core, 2 * order[(i + way) % size] + core))
        wide = lax.axis_index("wide")
        self.core = lax.axis_index("narrow")
        half = wide // 2
        self.place = jnp.where(wide % 2 == 0, half, size - 1 - half)
        self.way = 1 - 2 * self.core

    def send(self, value):
        return lax.ppermute(value, ("wide", "narrow"), self.pairs)

    def chunk(self, back):
        return lax.rem(self.place - self.way * back + 2 * self.size, self.size)


def collected(grad, core):
    taps, rows, width = grad.shape
    share = lax.psum_scatter(grad.reshape(-1, width), "wide", scatter_dimension=0, tiled=True)
    mine = lax.all_gather(share, "wide", axis=0, tiled=True).reshape(grad.shape)
    theirs = swap_cores(mine)
    lower, upper = jnp.where(core == 0, mine, theirs), jnp.where(core == 0, theirs, mine)
    return jnp.concatenate([lower, upper], 1)


class Lane:
    def __init__(self, parts, ring, low, stride, blocks):
        self.ring, self.low, self.stride, self.blocks = ring, low, stride, blocks
        self.held, self.parts = parts
        self.passed = [self.held]
        self.pieces, self.lows = [], []

    def keep(self, back):
        for piece, own in ((self.held, True), (swap_cores(self.held), False)):
            self.pieces.append(piece.reshape(9, -1, piece.shape[-1]))
            self.lows.append((self.low, self.stride, back, own))

    def step(self, number):
        last = self.ring.size - 1
        if number == last:
            self.keep(0)
        got = self.got = self.ring.send(self.held)
        if number < last:
            self.passed.append(got)
            if number < last - 1:
                self.held = got + self.parts[number]
            else:
                self.held = got[: self.blocks] + self.parts[number, : self.blocks]
        else:
            self.held = got
            self.keep(number - last + 1)


def lay_lanes(lanes, results, shapes):
    pieces, layout = [], []
    for lane, at in lanes:
        pieces += lane.pieces
        layout += [(at,) + low for low in lane.lows]
        size, lane.pieces, lane.lows = lane.ring.size, [], []
    return lay(size, pieces, layout, results, shapes)


def after(value, *others):
    return lax.optimization_barrier((value,) + others)[0]


def body(frames, weight3, bias3, weight4, bias4, cotangent, clip_counts):
    count, side, c_in = frames.shape[1], frames.shape[2], frames.shape[4]
    w_three, w_four = (weight3[0], weight4[0])
    c_mid, c_out = w_three.shape[1], w_four.shape[1]
    taps3, taps4 = w_three.reshape(9, c_in, c_mid), w_four.reshape(9, c_mid, c_out)
    size = lax.axis_size("wide")
    ring = Ring(size)
    core = ring.core
    total_frames = count * size * lax.axis_size("narrow")
    def cells_first(field):
        return jnp.transpose(field, (1, 2, 0, 3))

    def frames_first(field):
        return jnp.transpose(field, (2, 0, 1, 3))

    output, act_mine, slope3, delta4, field_mine, send = head(
        total_frames, clip_counts, cells_first(frames[0]), w_three, bias3, w_four, bias4,
        cells_first(cotangent[0]),
    )
    small = size <= 8
    chunks = size if small else 1
    lanes4 = 2 if small else 1
    theirs = swap_cores(send)
    delta3_sums, delta3, sums = back4(count, delta4, slope3, taps4)
    delta3_theirs = swap_cores(delta3_sums)
    grads4 = grad(
        62, side, count, lanes4, chunks, size, c_out,
        (after(act_mine, delta3), 0), (theirs, c_out), (delta4, 0), (theirs, 0),
    )
    def grad_of_3(mine, sums):
        return grad(
            24, side, count, 1, chunks, size, c_mid,
            (mine, 0), (theirs, c_out + c_mid // 2), (delta3, 0), (delta3_theirs, 0), sums,
        )[0]

    if not small:
        grads3 = grad_of_3(field_mine, ())
        biases = lax.psum(sums, ("wide", "narrow"))
        sum3, sum4 = biases[0:1], biases[1:2]
        grad_w4 = collected(grads4[0][0].reshape(9, -1, c_out), core)
        grad_w3 = collected(grads3[0].reshape(9, -1, c_mid), core)
    else:
        half3, half4, quarter = c_in // 2, c_mid // 2, c_mid // 4
        blocks = 9 * quarter // (8 * size)
        x = Lane(grads4[0], ring, 0, half4, blocks)
        y = Lane(grads4[1], ring, quarter, half4, blocks)
        x.step(0)
        y.step(0)
        grads3 = grad_of_3(field_mine, (sums,))
        z = Lane(grads3, ring, 0, half3, 9 * half3 // (8 * size))
        z.held = after(z.held, x.got, y.got)
        x.held, y.held = after(x.held, z.held), after(y.held, z.held)
        grad_w4 = grad_w3 = None
        shape3, shape4 = (9, c_in, c_mid), (9, c_mid, c_out)
        last = 2 * (size - 1) - 1
        for number in range(last + 1):
            if number == last - 4:
                (grad_w3,) = lay_lanes([(z, 0)], [grad_w3], [shape3])
            if number == last - 3:
                y.held = after(y.held, grad_w3)
                (grad_w4,) = lay_lanes([(y, 0)], [grad_w4], [shape4])
            if number == last - 2:
                x.held = after(x.held, grad_w4)
                (grad_w4,) = lay_lanes([(x, 0)], [grad_w4], [shape4])
            if number == last - 1:
                z.held = after(z.held, grad_w4)
                (grad_w3,) = lay_lanes([(z, 0)], [grad_w3], [shape3])
                (grad_w4,) = lay_lanes([(y, 0)], [grad_w4], [shape4])
            if number == last:
                y.held = after(y.held, grad_w3)
                x.held = after(x.held, grad_w4)
            z.step(number)
            if number > 0:
                y.step(number)
                x.step(number)
            if number == size - 1:
                sum3, sum4 = tally(z.passed)
            if number == size:
                x.held = after(x.held, sum3)
            if number == 3:
                field_grad = back3(side, count, after(delta3, z.held), taps3)
            if number == 5:
                z.held = after(z.held, field_grad)
        grad_w3, grad_w4 = lay_lanes([(z, 0), (y, 1)], [grad_w3, grad_w4], [shape3, shape4])
        (grad_w4,) = lay_lanes([(x, 0)], [grad_w4], [shape4])
    if not small:
        field_grad = back3(side, count, delta3, taps3)
    return (
        frames_first(output)[None],
        frames_first(field_grad)[None],
        grad_w3.reshape(w_three.shape)[None],
        sum3,
        grad_w4.reshape(w_four.shape)[None],
        sum4,
    )


def solution(mesh):
    return jax.shard_map(
        body,
        mesh=mesh,
        in_specs=(
            P("stream", ("wide", "narrow"), None, None, None),
            P("stream", None, None),
            P("stream", None),
            P("stream", None, None),
            P("stream", None),
            P("stream", ("wide", "narrow"), None, None, None),
            P(),
        ),
        out_specs=(
            P("stream", ("wide", "narrow"), None, None, None),
            P("stream", ("wide", "narrow"), None, None, None),
            P("stream", None, None),
            P("stream", None),
            P("stream", None, None),
            P("stream", None),
        ),
        check_vma=False,
    )
```
